256 devices in a mesh: dp: 32 (over y, z), hidden: 8 (over x, core).
Axes of the slice: x: 4, y: 4, z: 8, core: 2. Of those that a mesh axis runs over, the one named last changes fastest.
Arguments:
- tokens: bfloat16 [4096, 4096], P('dp'), may hold values from -6 to 6
- gate_weight: bfloat16 [4096, 14336], P('dp', 'hidden'), may hold values from -0.09375 to 0.09375
- up_weight: bfloat16 [4096, 14336], P('dp', 'hidden'), may hold values from -0.09375 to 0.09375
- cotangent: bfloat16 [4096, 4096], P('dp'), may hold values from -6 to 6
- query_left: bfloat16 [512, 14336], P(None, 'hidden'), may hold values from -0.046875 to 0.046875
- query_right: bfloat16 [512, 4096], P('hidden'), may hold values from -0.005859375 to 0.005859375
- doc_ids: int32 [4096], P('dp'), may hold values from 0 to 255, never falling along the last dimension, each value on 1 to 256 neighbouring positions
- doc_slot: int32 [256], replicated, may hold values from 0 to 255, each once
Outputs:
- doc_scores: float32 [16, 256], P('hidden', 'dp')
The draws below stay inside these ranges and needn't reach their ends.
Inputs may be any that keep to these rules, and one draw needn't show every extreme that they name: `doc_ids`: document numbers never fall along the 4096 tokens; every document has 1 to 256 tokens and one has exactly 256. `doc_slot`: each column is named by exactly one document.
All inputs are finite; a program needn't handle non-finite values.
Results may differ from the reference program's by a relative error of at most 0.0031.
Values may be sent and summed in bfloat16 or wider, within the bound.
A program may use at most 128 MiB of HBM per device.

```python
import math
import jax
import jax.numpy as jnp
import numpy as np
from jax import lax

D = 4096
FF = 14336
TOK_DEV = 128
Q = 16
R = 32
TOKENS = 4096
DOCS = 256
N_DP = 32


def shard_levels(rng, shape, split, smallest, largest):
    def one(dim, blocks):
        steps = jax.random.uniform(jax.random.fold_in(jax.random.fold_in(rng, 6), dim), (blocks,), jnp.float32, smallest / len(split), largest / len(split))
        return jnp.repeat(jnp.exp(steps), shape[dim] // blocks).reshape((-1,) + (1,) * (len(shape) - dim - 1))

    loudness = one(*split[0])
    for cut in split[1:]:
        loudness = loudness * one(*cut)
    return loudness


def length_profile(count, total, limit, slope):
    portions = [(1 << 20) // math.isqrt(grade ** slope) + 1 for grade in range(2, count + 1)]
    surplus, holding = total - limit - (count - 1), [1] * (count - 1)
    while surplus > 0:
        free = [i for i in range(count - 1) if holding[i] < limit]
        mass, left = sum([portions[i] for i in free]), surplus
        for i in free:
            addition = min(limit - holding[i], max(1, left * portions[i] // mass), surplus)
            holding[i] = holding[i] + addition
            surplus = surplus - addition
    return np.array([limit] + holding)


def ragged(rng, count, total, bound, lean):
    if count == 2:
        one = jax.random.randint(rng, (), max(1, total - bound), min(bound, total - 1) + 1)
        return jnp.stack([one, total - one])
    lengths = jnp.asarray(length_profile(count, total, bound, lean), jnp.int32)
    pairs = (count - 1) // 2
    donor, sink = lengths[1:1 + 2 * pairs:2], lengths[2:2 + 2 * pairs:2]
    slack = jnp.minimum(donor - 1, bound - sink)
    shifted = jax.random.randint(jax.random.fold_in(rng, 1), (pairs,), 0, 1 << 20) % (slack + 1)
    lengths = lengths.at[1:1 + 2 * pairs:2].set(donor - shifted).at[2:2 + 2 * pairs:2].set(sink + shifted)
    return lengths[jax.random.permutation(jax.random.fold_in(rng, 2), count)]


def scatter_about(stream_key, shape, scale, reach, pieces=(), kind=jnp.bfloat16):
    values = jax.random.normal(stream_key, shape, jnp.float32) * scale
    if len(pieces) > 0:
        values = shard_levels(stream_key, shape, pieces, -0.22, 0.18) * values
    return jnp.clip(values, min=-reach, max=reach).astype(kind)


def setup_inputs(seed: int = 0) -> dict:
    streams_of = jax.random.split(jax.random.key(seed), 9)
    tokens = scatter_about(streams_of[0], (TOKENS, D), 1.0, 6.0, ((0, 32),))
    gate_weight = scatter_about(streams_of[1], (D, FF), D ** -0.5, 0.09375, ((0, 32), (1, 8)))
    up_weight = scatter_about(streams_of[2], (D, FF), D ** -0.5, 0.09375, ((0, 32), (1, 8)))
    cotangent = scatter_about(streams_of[3], (TOKENS, D), 1.0, 6.0, ((0, 32),))
    query_left = scatter_about(streams_of[4], (Q * R, FF), FF ** -0.5, 0.046875, ((1, 8),))
    query_right = scatter_about(streams_of[5], (Q * R, D), (256 * D) ** -0.5, 0.005859375, ((0, 8),))
    doc_ids = jnp.searchsorted(jnp.cumsum(ragged(streams_of[6], DOCS, TOKENS, 2 * TOK_DEV, 2)), jnp.arange(TOKENS), side="right").astype(jnp.int32)
    doc_slot = jax.random.permutation(streams_of[7], DOCS).astype(jnp.int32)
    return dict(tokens=tokens, gate_weight=gate_weight, up_weight=up_weight, cotangent=cotangent, query_left=query_left, query_right=query_right, doc_ids=doc_ids, doc_slot=doc_slot)


def reference(tokens, gate_weight, up_weight, cotangent, query_left, query_right, doc_ids, doc_slot):
    token_groups = tokens.reshape(N_DP, TOK_DEV, D)
    grad_groups = cotangent.reshape(N_DP, TOK_DEV, D)
    id_groups = doc_ids.reshape(N_DP, TOK_DEV)
    contract_dims = (((1,), (1,)), ((), ()))
    doc_range = jnp.arange(DOCS, dtype=jnp.int32)

    def one_window(running, group_item):
        window, window_grad, window_ids = group_item
        gate = jnp.dot(window, gate_weight, preferred_element_type=jnp.float32)
        up_part = jnp.dot(window, up_weight, preferred_element_type=jnp.float32)
        hidden_act = (jax.nn.silu(gate) * up_part).astype(jnp.bfloat16)
        left_proj = lax.dot_general(query_left, hidden_act, contract_dims, preferred_element_type=jnp.float32)
        right_proj = lax.dot_general(query_right, window_grad, contract_dims, preferred_element_type=jnp.float32)
        token_scores = (left_proj * right_proj).reshape(Q, R, TOK_DEV).sum(axis=1)
        one_hot = (window_ids[:, None] == doc_range[None, :]).astype(jnp.float32)
        by_doc = jnp.dot(token_scores, one_hot, precision=lax.Precision.HIGHEST)
        return running + by_doc, None

    start_value = jnp.zeros((Q, DOCS), jnp.float32)
    by_doc, _ = lax.scan(one_window, start_value, (token_groups, grad_groups, id_groups))
    placing = (doc_slot[:, None] == doc_range[None, :]).astype(jnp.float32)
    return jnp.dot(by_doc, placing, precision=lax.Precision.HIGHEST)
```

```python
import jax
import jax.numpy as jnp
from jax import lax
from jax.sharding import PartitionSpec as P

R = 32
NY, NZ = 4, 8
Z_GROUPS = [[y * NZ + z for z in range(NZ)] for y in range(NY)]
Y_GROUPS = [[y * NZ + z for y in range(NY)] for z in range(NZ)]


def local(tokens, gate_weight, up_weight, cotangent, query_left, query_right, doc_ids, doc_slot):
    contract_last = (((1,), (1,)), ((), ()))
    hidden = lax.axis_index("hidden")
    z = lax.rem(lax.axis_index("dp"), NZ)
    rows, units = gate_weight.shape
    part = units // NZ
    both = jnp.stack([gate_weight.T, up_weight.T]).reshape(2, NZ, part, rows)
    mixed = lax.all_to_all(both, "dp", 1, 1, axis_index_groups=Z_GROUPS, tiled=True)
    weights = lax.all_gather(mixed, "dp", axis=0, axis_index_groups=Y_GROUPS)
    weights = weights.transpose(1, 3, 0, 2, 4).reshape(2 * part, NY * NZ * rows)

    count = tokens.shape[0] // 8
    piece = lax.dynamic_slice_in_dim(tokens, hidden * count, count, 0)
    pieces = lax.all_gather(piece, "dp", axis=0, axis_index_groups=Z_GROUPS)
    window = lax.all_gather(pieces, "hidden", axis=1).reshape(NZ * tokens.shape[0], -1)

    pre = lax.dot_general(weights, window, contract_last, preferred_element_type=jnp.float32)
    hidden_act = (jax.nn.silu(pre[:part]) * pre[part:]).astype(jnp.bfloat16)
    left = lax.dynamic_slice_in_dim(query_left, z * part, part, 1)
    partial_proj = jnp.dot(left, hidden_act, preferred_element_type=jnp.float32)

    right = lax.dot_general(query_right, cotangent, contract_last, preferred_element_type=jnp.float32)
    right = lax.all_gather(right, "hidden", axis=0, tiled=True)
    right = lax.all_gather(right, "dp", axis=1, axis_index_groups=Z_GROUPS, tiled=True)
    ids = lax.all_gather(doc_ids, "dp", axis=0, axis_index_groups=Z_GROUPS, tiled=True)
    queries = partial_proj.shape[0] // R
    token_scores = (partial_proj * right).reshape(queries, R, -1).sum(axis=1)
    doc_range = jnp.arange(doc_slot.shape[0], dtype=jnp.int32)
    one_hot = (ids[:, None] == doc_range[None, :]).astype(jnp.float32)
    by_doc = jnp.dot(token_scores, one_hot, precision=lax.Precision.HIGHEST)
    placing = (doc_slot[:, None] == doc_range[None, :]).astype(jnp.float32)
    by_column = jnp.dot(by_doc, placing, precision=lax.Precision.HIGHEST)
    mine = lax.psum_scatter(by_column, "hidden", scatter_dimension=0, tiled=True)
    return lax.psum_scatter(mine, "dp", scatter_dimension=1, tiled=True)


def solution(mesh):
    return jax.shard_map(
        local,
        mesh=mesh,
        in_specs=(
            P("dp", None),
            P("dp", "hidden"),
            P("dp", "hidden"),
            P("dp", None),
            P(None, "hidden"),
            P("hidden", None),
            P("dp"),
            P(),
        ),
        out_specs=P("hidden", "dp"),
        check_vma=False,
    )
```

```python
import jax
import jax.numpy as jnp
from jax import lax
from jax.experimental import pallas as pl
from jax.experimental.pallas import tpu as pltpu
from jax.sharding import PartitionSpec as P

MESH = pl.DeviceIdType.MESH
NT = (((1,), (1,)), ((), ()))
NX, NY, NZ = 4, 4, 8
R = 32
F = 224
DIST = (0, -1, 1, -2, 2, -3, 3, 4)
PLACE = {d: i for i, d in enumerate(DIST)}
PLACE[-4] = PLACE[4]


def kernel(
    tokens, gate, up, cot, ql, qr, ids, slot, out,
    tok, wb, rb, idb, gate_v, up_v, gate_t, up_t, cot_v, qr_v, ql_v, ids_v, slot_v,
    acc, act, scores, spread, part, got, tile, tiles,
    local_sem, z_send, x_send, c_send, w_send, y_send, r_send, tail_send,
    z_recv, x_recv, xh_recv, c_recv, w_recv, y_recv, yh_recv, rz_recv, rx_recv, rc_recv, tail_recv,
):
    dp, hid = lax.axis_index("dp"), lax.axis_index("hidden")
    y, z = dp // NZ, lax.rem(dp, NZ)
    x, c = hid // 2, lax.rem(hid, 2)
    hidden_count = 2 * NX

    def at(dx=0, dy=0, dz=0, dc=0):
        return (
            lax.rem(y + dy + NY, NY) * NZ + lax.rem(z + dz + NZ, NZ),
            lax.rem(x + dx + NX, NX) * 2 + lax.rem(c + dc, 2),
        )

    def send(src, dst, send_sem, recv_sem, **where):
        pltpu.make_async_remote_copy(
            src, dst, send_sem, recv_sem, device_id=at(**where), device_id_type=MESH
        ).start()

    def wait(ref, sem):
        pltpu.make_async_copy(ref, ref, sem).wait()

    loads = [
        pltpu.make_async_copy(gate, gate_v, local_sem.at[0]),
        pltpu.make_async_copy(up, up_v, local_sem.at[1]),
        pltpu.make_async_copy(cot, cot_v, local_sem.at[2]),
        pltpu.make_async_copy(qr, qr_v, local_sem.at[3]),
        pltpu.make_async_copy(ids, ids_v, local_sem.at[4]),
        pltpu.make_async_copy(slot, slot_v, local_sem.at[5]),
        pltpu.make_async_copy(
            ql.at[:, pl.ds(pl.multiple_of((5 * z) // 3 * 128, 128), 384)], ql_v, local_sem.at[6]
        ),
        pltpu.make_async_copy(tokens, tok.at[pl.ds(0, 128)], local_sem.at[7]),
    ]
    for load in loads:
        load.start()

    barrier = pltpu.get_barrier_semaphore()
    peers = [dict(dz=d) for d in range(1, NZ)] + [dict(dx=d) for d in range(1, NX)]
    peers += [dict(dy=1), dict(dy=-1), dict(dc=1)]
    for peer in peers:
        pl.semaphore_signal(barrier, inc=1, device_id=at(**peer), device_id_type=MESH)
    pl.semaphore_wait(barrier, len(peers))

    def rows(d, dx=0):
        first = c * 64 + lax.rem(x + dx + NX, NX) * 16
        return pl.ds(pl.multiple_of(PLACE[d] * 128 + first, 16), 16)

    half = (pl.ds(0, 2048), pl.ds(2048, 2048))
    own_rows = pl.ds(pl.multiple_of(c * 64 + x * 16, 16), 16)
    for s in (1, -1):
        send(tokens.at[own_rows], tok.at[rows(-s)], z_send, z_recv.at[PLACE[-s]], dz=s)

    loads[0].wait()
    loads[1].wait()

    @pl.loop(0, 14)
    def _(i):
        at_tile = pl.ds(pl.multiple_of(i * 128, 128), 128)
        gate_t[at_tile, :] = gate_v[:, at_tile].T
        up_t[at_tile, :] = up_v[:, at_tile].T

    def window(dz=0, dy=0):
        return lax.rem(y + dy + NY, NY) * NZ + lax.rem(z + dz + NZ, NZ)

    def units(dz):
        return pl.ds(pl.multiple_of(lax.rem(z + dz + NZ, NZ) * F, 32), F)

    upper, lower = pl.ds(0, F), pl.ds(F, F)
    for s in (1, -1):
        send(gate_t.at[units(0)], wb.at[dp, upper], y_send, y_recv.at[0, (1 - s) // 2], dy=s)
        send(up_t.at[units(0)], wb.at[dp, lower], y_send, y_recv.at[0, (1 - s) // 2], dy=s)
    for d in (1, -1, 2, -2, 3, -3, 4):
        send(gate_t.at[units(d)], wb.at[dp, upper], w_send, w_recv.at[PLACE[-d]], dz=d)
        send(up_t.at[units(d)], wb.at[dp, lower], w_send, w_recv.at[PLACE[-d]], dz=d)
    wb[dp, upper, :] = gate_t[units(0), :]
    wb[dp, lower, :] = up_t[units(0), :]

    loads[2].wait()
    loads[3].wait()
    query_rows = pl.ds(pl.multiple_of(hid * 64, 64), 64)

    def k_rows(dx=0, dc=0):
        first = lax.rem(c + dc, 2) * 256 + lax.rem(x + dx + NX, NX) * 64
        return pl.ds(pl.multiple_of(first, 64), 64)

    rb[0, k_rows(), :] = lax.dot_general(
        qr_v[...], cot_v[...], NT, preferred_element_type=jnp.float32
    )
    loads[4].wait()
    idb[0] = ids_v[...]
    for d in (1, -1, 2, -2, 3, -3, 4):
        send(rb.at[0, k_rows()], rb.at[PLACE[-d], k_rows()], r_send.at[0], rz_recv.at[PLACE[-d]], dz=d)
        send(ids_v, idb.at[PLACE[-d]], r_send.at[1], rz_recv.at[PLACE[-d] + NZ], dz=d)

    def right_along_x(place):
        for d in (1, -1, 2):
            send(rb.at[place, k_rows()], rb.at[place, k_rows()], r_send.at[2], rx_recv.at[place], dx=d)

    def tokens_along_x(d):
        for s in (1, -1):
            send(tok.at[rows(d)], tok.at[rows(d)], x_send, x_recv.at[PLACE[d], (1 - s) // 2], dx=s)

    def pass_tokens(d):
        for s in (1, -1):
            i = (1 - s) // 2
            wait(tok.at[rows(d)], x_recv.at[PLACE[d], i])
            piece = tok.at[rows(d, -s), half[i]]
            send(piece, piece, x_send, xh_recv.at[PLACE[d], i], dx=s)

    def swap_cores(d):
        place = PLACE[d]
        for i in range(2):
            wait(tok.at[rows(d), half[i]], xh_recv.at[place, i])
        mine = tok.at[pl.ds(pl.multiple_of(place * 128 + c * 64, 16), 64)]
        send(mine, mine, c_send.at[0], c_recv.at[place], dc=1)
        wait(rb.at[place, pl.ds(0, 192)], rx_recv.at[place])
        mine = rb.at[place, pl.ds(pl.multiple_of(c * 256, 256), 256)]
        send(mine, mine, c_send.at[1], rc_recv.at[place], dc=1)

    def weights_along_y(d):
        piece = wb.at[window(d)]
        for s in (1, -1):
            send(piece, piece, y_send, y_recv.at[PLACE[d], (1 - s) // 2], dy=s)

    def pass_weights(d):
        for s in (1, -1):
            i = (1 - s) // 2
            wait(wb.at[dp], y_recv.at[PLACE[d], i])
            piece = wb.at[window(d, -s), (upper, lower)[i]]
            send(piece, piece, y_send, yh_recv.at[PLACE[d], i], dy=s)

    right_along_x(0)
    for g in range(1, 7):
        for d in (-g, g):
            if g < 4:
                s = 1 if d < 0 else -1
                place = PLACE[d]
                wait(tok.at[rows(d)], z_recv.at[place])
                if g < 3:
                    send(tok.at[rows(d)], tok.at[rows(d - s)], z_send, z_recv.at[PLACE[d - s]], dz=s)
                else:
                    i = (1 - s) // 2
                    send(
                        tok.at[rows(d), half[i]], tok.at[rows(4), half[i]], z_send,
                        z_recv.at[NZ - 1 + i], dz=s,
                    )
                tokens_along_x(d)
        if g == 4:
            for i in range(2):
                wait(tok.at[rows(4), half[i]], z_recv.at[NZ - 1 + i])
            tokens_along_x(4)
        for d in (-g, g) if g < 4 else (4,) if g == 4 else ():
            wait(wb.at[dp], w_recv.at[PLACE[d]])
            weights_along_y(d)
        for d in (-g, g) if g < 4 else (4,) if g == 4 else ():
            wait(rb.at[0, pl.ds(0, 64)], rz_recv.at[PLACE[d]])
            wait(idb.at[0], rz_recv.at[PLACE[d] + NZ])
            right_along_x(PLACE[d])
        h = g - 1
        for d in (0,) if h == 0 else (-h, h) if h < 4 else (4,) if h == 4 else ():
            pass_weights(d)
            if h > 0:
                pass_tokens(d)
        h = g - 2
        for d in (-h, h) if 0 < h < 4 else (4,) if h == 4 else ():
            swap_cores(d)

    loads[5].wait()
    columns = lax.broadcasted_iota(jnp.int32, (256, 256), 0)
    placing = (columns == slot_v[...]).astype(jnp.float32).astype(jnp.bfloat16)
    docs = lax.broadcasted_iota(jnp.int32, (256, 128), 0)
    for place in range(NZ):
        one_hot = (docs == idb[place]).astype(jnp.float32).astype(jnp.bfloat16)
        spread[:, pl.ds(place * 128, 128)] = jnp.dot(
            placing, one_hot, preferred_element_type=jnp.float32
        ).astype(jnp.bfloat16)

    wait(rb.at[0, pl.ds(0, 192)], rx_recv.at[0])
    mine = rb.at[0, pl.ds(pl.multiple_of(c * 256, 256), 256)]
    send(mine, mine, c_send.at[1], rc_recv.at[0], dc=1)
    for d in DIST:
        for i in range(2):
            wait(wb.at[dp, upper], yh_recv.at[PLACE[d], i])
        if d != 0:
            wait(tok.at[pl.ds(0, 64)], c_recv.at[PLACE[d]])
        wait(rb.at[0, pl.ds(0, 256)], rc_recv.at[PLACE[d]])
    loads[6].wait()
    loads[7].wait()
    act[...] = jnp.zeros_like(act)
    scores[...] = jnp.zeros_like(scores)
    first = pl.multiple_of(F * z - (5 * z) // 3 * 128, 32)

    @pl.loop(0, 4)
    def _(j):
        span = pl.ds(pl.multiple_of(j * 256, 256), 256)
        acc[...] = jnp.zeros_like(acc)

        @pl.loop(0, 4)
        def _(k):
            weights = jnp.concatenate([wb[k * 8 + i] for i in range(8)], axis=1)
            inputs = tok[span, pl.ds(pl.multiple_of(k * 1024, 1024), 1024)]
            acc[...] += lax.dot_general(weights, inputs, NT, preferred_element_type=jnp.float32)

        gates = acc[:F]
        act[pl.ds(first, F), :] = (gates / (1.0 + jnp.exp(-gates)) * acc[F:]).astype(jnp.bfloat16)
        left = jnp.dot(ql_v[...], act[...], preferred_element_type=jnp.float32)
        for q in range(16):
            where = (q % 4 // 2 * 64 + q % 2 * 32) + (q // 4) * 128
            hidden = where // 64
            at_row = hidden % 2 * 256 + hidden // 2 * 64 + where % 64
            right = jnp.concatenate(
                [rb[2 * j, at_row:at_row + R], rb[2 * j + 1, at_row:at_row + R]], axis=1
            )
            scores[q:q + 1, span] = jnp.sum(
                left[q * R:(q + 1) * R] * right, axis=0, keepdims=True
            )

    rest = scores[...]
    columns_sum = jnp.zeros((256, 128), jnp.float32)
    for _ in range(3):
        rounded = rest.astype(jnp.bfloat16)
        rest = rest - rounded.astype(jnp.float32)
        columns_sum += lax.dot_general(spread[...], rounded, NT, preferred_element_type=jnp.float32)
    part[...] = columns_sum.reshape(32, 8, 128)

    @pl.loop(1, 32)
    def _(k):
        to = lax.rem(dp + k, 32)
        pltpu.make_async_remote_copy(
            part.at[to], got.at[dp], tail_send.at[0], tail_recv.at[0],
            device_id=(to, hid), device_id_type=MESH,
        ).start()

    wait(got.at[pl.ds(0, 31)], tail_recv.at[0])
    got[dp] = part[dp]
    tile[...] = jnp.sum(got[...], axis=0)
    for k in range(1, hidden_count):
        pltpu.make_async_remote_copy(
            tile, tiles.at[hid], tail_send.at[1], tail_recv.at[1],
            device_id=(dp, lax.rem(hid + k, hidden_count)), device_id_type=MESH,
        ).start()
    wait(tiles.at[pl.ds(0, hidden_count - 1)], tail_recv.at[1])
    tiles[hid] = tile[...]
    total = jnp.sum(tiles[...], axis=0)
    query = lax.broadcasted_iota(jnp.int32, (8, 128), 0) + 2 * hid
    pick = (lax.broadcasted_iota(jnp.int32, (8, 128), 1) == query).astype(jnp.float32)
    result = lax.dot_general(
        pick, total, NT, precision=lax.Precision.HIGHEST, preferred_element_type=jnp.float32
    )
    out[...] = result[:2]

    wait(tok.at[pl.ds(0, 7 * 16)], z_send)
    wait(tok.at[pl.ds(0, 7 * 48)], x_send)
    wait(tok.at[pl.ds(0, 7 * 64)], c_send.at[0])
    wait(rb.at[:, pl.ds(0, 256)], c_send.at[1])
    wait(wb.at[pl.ds(0, 7)], w_send)
    wait(wb.at[pl.ds(0, 24)], y_send)
    wait(rb.at[pl.ds(0, 7), pl.ds(0, 64)], r_send.at[0])
    wait(idb.at[pl.ds(0, 7)], r_send.at[1])
    wait(rb.at[:, pl.ds(0, 192)], r_send.at[2])
    wait(got.at[pl.ds(0, 31)], tail_send.at[0])
    wait(tiles.at[pl.ds(0, hidden_count - 1)], tail_send.at[1])


def local(tokens, gate_weight, up_weight, cotangent, query_left, query_right, doc_ids, doc_slot):
    bf16, f32, i32 = jnp.bfloat16, jnp.float32, jnp.int32
    dma = pltpu.SemaphoreType.DMA
    anywhere = pl.BlockSpec(memory_space=pl.ANY)
    return pl.pallas_call(
        kernel,
        out_shape=jax.ShapeDtypeStruct((2, 8), f32),
        in_specs=[anywhere] * 8,
        out_specs=pl.BlockSpec(memory_space=pltpu.VMEM),
        scratch_shapes=[
            pltpu.VMEM((1024, 4096), bf16),
            pltpu.VMEM((32, 2 * F, 128), bf16),
            pltpu.VMEM((8, 512, 128), f32),
            pltpu.VMEM((8, 1, 128), i32),
            pltpu.VMEM((128, 1792), bf16),
            pltpu.VMEM((128, 1792), bf16),
            pltpu.VMEM((1792, 128), bf16),
            pltpu.VMEM((1792, 128), bf16),
            pltpu.VMEM((128, 4096), bf16),
            pltpu.VMEM((64, 4096), bf16),
            pltpu.VMEM((512, 384), bf16),
            pltpu.VMEM((1, 128), i32),
            pltpu.VMEM((1, 256), i32),
            pltpu.VMEM((2 * F, 256), f32),
            pltpu.VMEM((384, 256), bf16),
            pltpu.VMEM((128, 1024), f32),
            pltpu.VMEM((256, 1024), bf16),
            pltpu.VMEM((32, 8, 128), f32),
            pltpu.VMEM((32, 8, 128), f32),
            pltpu.VMEM((8, 128), f32),
            pltpu.VMEM((8, 8, 128), f32),
            dma((8,)), dma, dma, dma((2,)), dma, dma, dma((3,)), dma((2,)),
            dma((9,)), dma((8, 2)), dma((8, 2)), dma((8,)), dma((8,)), dma((8, 2)), dma((8, 2)),
            dma((16,)), dma((8,)), dma((8,)), dma((2,)),
        ],
        compiler_params=pltpu.CompilerParams(
            collective_id=0, has_side_effects=True, vmem_limit_bytes=48 * 1024 * 1024
        ),
        name="influence",
    )(
        tokens, gate_weight, up_weight, cotangent, query_left, query_right,
        doc_ids.reshape(1, -1), doc_slot.reshape(1, -1),
    )


def solution(mesh):
    return jax.shard_map(
        local,
        mesh=mesh,
        in_specs=(
            P("dp", None),
            P("dp", "hidden"),
            P("dp", "hidden"),
            P("dp", None),
            P(None, "hidden"),
            P("hidden", None),
            P("dp"),
            P(),
        ),
        out_specs=P("hidden", "dp"),
        check_vma=False,
    )
```

```python
import jax
import jax.numpy as jnp
from jax import lax
from jax.experimental import pallas as pl
from jax.experimental.pallas import tpu as pltpu
from jax.sharding import PartitionSpec as P

MESH = pl.DeviceIdType.MESH
NT = (((1,), (1,)), ((), ()))
NX, NY, NZ = 4, 4, 8
R = 32
F = 224
DIST = (0, -1, 1, -2, 2, -3, 3, 4)
PLACE = {d: i for i, d in enumerate(DIST)}
PLACE[-4] = PLACE[4]


def kernel(
    tokens, gate, up, cot, ql, qr, ids, slot, out,
    tok, wb, rb, sb, idb, gate_v, up_v, gate_t, up_t, cot_v, qr_v, ql_v, ids_v, slot_v,
    acc, act, scores, spread, part, got, tile, tiles,
    local_sem, z_send, x_send, c_send, w_send, y_send, r_send, tail_send,
    z_recv, x_recv, xh_recv, c_recv, w_recv, y_recv, yh_recv,
    rz_recv, rx_recv, rxh_recv, rc_recv, tail_recv,
):
    dp, hid = lax.axis_index("dp"), lax.axis_index("hidden")
    y, z = dp // NZ, lax.rem(dp, NZ)
    x, c = hid // 2, lax.rem(hid, 2)
    hidden_count = 2 * NX

    def at(dx=0, dy=0, dz=0, dc=0):
        return (
            lax.rem(y + dy + NY, NY) * NZ + lax.rem(z + dz + NZ, NZ),
            lax.rem(x + dx + NX, NX) * 2 + lax.rem(c + dc, 2),
        )

    def send(src, dst, send_sem, recv_sem, **where):
        pltpu.make_async_remote_copy(
            src, dst, send_sem, recv_sem, device_id=at(**where), device_id_type=MESH
        ).start()

    def wait(ref, sem):
        pltpu.make_async_copy(ref, ref, sem).wait()

    loads = [
        pltpu.make_async_copy(gate, gate_v, local_sem.at[0]),
        pltpu.make_async_copy(up, up_v, local_sem.at[1]),
        pltpu.make_async_copy(cot, cot_v, local_sem.at[2]),
        pltpu.make_async_copy(qr, qr_v, local_sem.at[3]),
        pltpu.make_async_copy(ids, ids_v, local_sem.at[4]),
        pltpu.make_async_copy(slot, slot_v, local_sem.at[5]),
        pltpu.make_async_copy(
            ql.at[:, pl.ds(pl.multiple_of((5 * z) // 3 * 128, 128), 384)], ql_v, local_sem.at[6]
        ),
        pltpu.make_async_copy(tokens, tok.at[pl.ds(0, 128)], local_sem.at[7]),
    ]
    for load in loads:
        load.start()

    barrier = pltpu.get_barrier_semaphore()
    peers = [dict(dz=1), dict(dz=-1), dict(dx=1), dict(dx=-1), dict(dy=1), dict(dy=-1), dict(dc=1)]
    for peer in peers:
        pl.semaphore_signal(barrier, inc=1, device_id=at(**peer), device_id_type=MESH)
    pl.semaphore_wait(barrier, len(peers))

    def rows(d, dx=0):
        first = c * 64 + lax.rem(x + dx + NX, NX) * 16
        return pl.ds(pl.multiple_of(PLACE[d] * 128 + first, 16), 16)

    half = (pl.ds(0, 2048), pl.ds(2048, 2048))
    own_rows = pl.ds(pl.multiple_of(c * 64 + x * 16, 16), 16)
    for s in (1, -1):
        send(tokens.at[own_rows], tok.at[rows(-s)], z_send, z_recv.at[PLACE[-s]], dz=s)

    loads[0].wait()
    loads[1].wait()

    @pl.loop(0, 14)
    def _(i):
        at_tile = pl.ds(pl.multiple_of(i * 128, 128), 128)
        gate_t[at_tile, :] = gate_v[:, at_tile].T
        up_t[at_tile, :] = up_v[:, at_tile].T

    def window(dz=0, dy=0):
        return lax.rem(y + dy + NY, NY) * NZ + lax.rem(z + dz + NZ, NZ)

    def units(dz):
        return pl.ds(pl.multiple_of(lax.rem(z + dz + NZ, NZ) * F, 32), F)

    upper, lower = pl.ds(0, F), pl.ds(F, F)

    def exchange_weights(d):
        send(gate_t.at[units(d)], wb.at[dp, upper], w_send, w_recv.at[PLACE[-d]], dz=d)
        send(up_t.at[units(d)], wb.at[dp, lower], w_send, w_recv.at[PLACE[-d]], dz=d)

    for s in (1, -1):
        send(gate_t.at[units(0)], wb.at[dp, upper], y_send, y_recv.at[0, (1 - s) // 2], dy=s)
        send(up_t.at[units(0)], wb.at[dp, lower], y_send, y_recv.at[0, (1 - s) // 2], dy=s)
    for d in (1, -1):
        exchange_weights(d)
    wb[dp, upper, :] = gate_t[units(0), :]
    wb[dp, lower, :] = up_t[units(0), :]

    loads[2].wait()
    loads[3].wait()

    def k_rows(dx=0, first=0, count=64):
        start = c * 256 + lax.rem(x + dx + NX, NX) * 64 + first
        return pl.ds(pl.multiple_of(start, count), count)

    def scale_row(dx=0):
        return pl.ds(c * 4 + lax.rem(x + dx + NX, NX), 1)

    right = lax.dot_general(qr_v[...], cot_v[...], NT, preferred_element_type=jnp.float32)
    largest = jnp.maximum(jnp.max(jnp.abs(right), axis=0, keepdims=True), 1e-30)
    steps = right * (32000.0 / largest)
    steps = steps + jnp.where(steps >= 0, 0.5, -0.5)
    rb[0, k_rows(), :] = steps.astype(jnp.int32).astype(jnp.int16)
    sb[0, c * 4 + x] = largest / 32000.0
    loads[4].wait()
    idb[0] = ids_v[...]

    def right_along_z(d, s):
        to = PLACE[d - s]
        here = PLACE[d]
        send(rb.at[here, k_rows()], rb.at[to, k_rows()], r_send.at[0], rz_recv.at[0, to], dz=s)
        send(sb.at[here, scale_row()], sb.at[to, scale_row()], r_send.at[1], rz_recv.at[1, to], dz=s)
        send(idb.at[here], idb.at[to], r_send.at[2], rz_recv.at[2, to], dz=s)

    def group(g):
        return (0,) if g == 0 else (4,) if g == 4 else (-g, g)

    def places(g):
        return pl.ds(PLACE[group(g)[0]], len(group(g)))

    def right_along_x(g):
        for s in (1, -1):
            i = (1 - s) // 2
            mine = rb.at[places(g), k_rows()]
            send(mine, mine, r_send.at[3], rx_recv.at[0, g, i], dx=s)
            mine = sb.at[places(g), scale_row()]
            send(mine, mine, r_send.at[4], rx_recv.at[1, g, i], dx=s)

    def pass_right(g):
        for s in (1, -1):
            i = (1 - s) // 2
            wait(rb.at[places(g), k_rows(-s)], rx_recv.at[0, g, i])
            wait(sb.at[places(g), scale_row(-s)], rx_recv.at[1, g, i])
            piece = rb.at[places(g), k_rows(-s, 32 * i, 32)]
            send(piece, piece, r_send.at[5], rxh_recv.at[i, g], dx=s)
        piece = sb.at[places(g), scale_row(-1)]
        send(piece, piece, r_send.at[6], rxh_recv.at[2, g], dx=1)

    def swap_right(g):
        for i in range(2):
            wait(rb.at[places(g), k_rows(2, 32 * i, 32)], rxh_recv.at[i, g])
        wait(sb.at[places(g), scale_row(2)], rxh_recv.at[2, g])
        mine = rb.at[places(g), pl.ds(pl.multiple_of(c * 256, 256), 256)]
        send(mine, mine, c_send.at[1], rc_recv.at[0, g], dc=1)
        mine = sb.at[places(g), pl.ds(c * 4, 4)]
        send(mine, mine, c_send.at[2], rc_recv.at[1, g], dc=1)

    def tokens_along_x(d):
        for s in (1, -1):
            send(tok.at[rows(d)], tok.at[rows(d)], x_send, x_recv.at[PLACE[d], (1 - s) // 2], dx=s)

    def pass_tokens(d):
        for s in (1, -1):
            i = (1 - s) // 2
            wait(tok.at[rows(d)], x_recv.at[PLACE[d], i])
            piece = tok.at[rows(d, -s), half[i]]
            send(piece, piece, x_send, xh_recv.at[PLACE[d], i], dx=s)

    def swap_cores(d):
        place = PLACE[d]
        for i in range(2):
            wait(tok.at[rows(d), half[i]], xh_recv.at[place, i])
        mine = tok.at[pl.ds(pl.multiple_of(place * 128 + c * 64, 16), 64)]
        send(mine, mine, c_send.at[0], c_recv.at[place], dc=1)

    def weights_along_y(d):
        piece = wb.at[window(d)]
        for s in (1, -1):
            send(piece, piece, y_send, y_recv.at[PLACE[d], (1 - s) // 2], dy=s)

    def pass_weights(d):
        for s in (1, -1):
            i = (1 - s) // 2
            wait(wb.at[dp], y_recv.at[PLACE[d], i])
            piece = wb.at[window(d, -s), (upper, lower)[i]]
            send(piece, piece, y_send, yh_recv.at[PLACE[d], i], dy=s)

    for s in (1, -1):
        right_along_z(0, s)
    right_along_x(0)
    for g in range(1, 7):
        if g < 4:
            for d in group(g):
                s = 1 if d < 0 else -1
                place = PLACE[d]
                wait(tok.at[rows(d)], z_recv.at[place])
                if g < 3:
                    send(tok.at[rows(d)], tok.at[rows(d - s)], z_send, z_recv.at[PLACE[d - s]], dz=s)
                else:
                    i = (1 - s) // 2
                    send(
                        tok.at[rows(d), half[i]], tok.at[rows(4), half[i]], z_send,
                        z_recv.at[NZ - 1 + i], dz=s,
                    )
                tokens_along_x(d)
            for d in group(g + 1):
                exchange_weights(d)
        if g == 4:
            for i in range(2):
                wait(tok.at[rows(4), half[i]], z_recv.at[NZ - 1 + i])
            tokens_along_x(4)
        if g <= 4:
            for d in group(g):
                for i in range(3):
                    wait((rb.at[0, k_rows()], sb.at[0, scale_row()], idb.at[0])[i], rz_recv.at[i, PLACE[d]])
                s = 1 if d < 0 else -1
                if g < 3 or d == -3:
                    right_along_z(d, s)
            right_along_x(g)
            for d in group(g):
                wait(wb.at[dp], w_recv.at[PLACE[d]])
                weights_along_y(d)
        h = g - 1
        if h <= 4:
            for d in group(h):
                pass_weights(d)
                if h > 0:
                    pass_tokens(d)
            pass_right(h)
        h = g - 2
        if 0 <= h <= 4:
            if h > 0:
                for d in group(h):
                    swap_cores(d)
            swap_right(h)

    loads[5].wait()
    columns = lax.broadcasted_iota(jnp.int32, (256, 256), 0)
    placing = (columns == slot_v[...]).astype(jnp.float32).astype(jnp.bfloat16)
    docs = lax.broadcasted_iota(jnp.int32, (256, 128), 0)
    for place in range(NZ):
        one_hot = (docs == idb[place]).astype(jnp.float32).astype(jnp.bfloat16)
        spread[:, pl.ds(place * 128, 128)] = jnp.dot(
            placing, one_hot, preferred_element_type=jnp.float32
        ).astype(jnp.bfloat16)

    for d in DIST:
        for i in range(2):
            wait(wb.at[dp, upper], yh_recv.at[PLACE[d], i])
        if d != 0:
            wait(tok.at[pl.ds(0, 64)], c_recv.at[PLACE[d]])
    for g in range(5):
        wait(rb.at[places(g), pl.ds(0, 256)], rc_recv.at[0, g])
        wait(sb.at[places(g), pl.ds(0, 4)], rc_recv.at[1, g])
    loads[6].wait()
    loads[7].wait()
    act[...] = jnp.zeros_like(act)
    scores[...] = jnp.zeros_like(scores)
    first = pl.multiple_of(F * z - (5 * z) // 3 * 128, 32)

    @pl.loop(0, 4)
    def _(j):
        span = pl.ds(pl.multiple_of(j * 256, 256), 256)
        acc[...] = jnp.zeros_like(acc)

        @pl.loop(0, 4)
        def _(k):
            weights = jnp.concatenate([wb[k * 8 + i] for i in range(8)], axis=1)
            inputs = tok[span, pl.ds(pl.multiple_of(k * 1024, 1024), 1024)]
            acc[...] += lax.dot_general(weights, inputs, NT, preferred_element_type=jnp.float32)

        gates = acc[:F]
        act[pl.ds(first, F), :] = (gates / (1.0 + jnp.exp(-gates)) * acc[F:]).astype(jnp.bfloat16)
        left = jnp.dot(ql_v[...], act[...], preferred_element_type=jnp.float32)
        for q in range(16):
            hidden = q // 2
            at_row = hidden % 2 * 256 + hidden // 2 * 64 + q % 2 * R
            right = jnp.concatenate(
                [
                    rb[2 * j + i, at_row:at_row + R].astype(jnp.int32).astype(jnp.float32)
                    * sb[2 * j + i, hidden % 2 * 4 + hidden // 2]
                    for i in range(2)
                ],
                axis=1,
            )
            scores[q:q + 1, span] = jnp.sum(
                left[q * R:(q + 1) * R] * right, axis=0, keepdims=True
            )

    rest = scores[...]
    columns_sum = jnp.zeros((256, 128), jnp.float32)
    for _ in range(3):
        rounded = rest.astype(jnp.bfloat16)
        rest = rest - rounded.astype(jnp.float32)
        columns_sum += lax.dot_general(spread[...], rounded, NT, preferred_element_type=jnp.float32)
    part[...] = columns_sum.reshape(32, 8, 128)

    @pl.loop(1, 32)
    def _(k):
        to = lax.rem(dp + k, 32)
        pltpu.make_async_remote_copy(
            part.at[to], got.at[dp], tail_send.at[0], tail_recv.at[0],
            device_id=(to, hid), device_id_type=MESH,
        ).start()

    wait(got.at[pl.ds(0, 31)], tail_recv.at[0])
    got[dp] = part[dp]
    tile[...] = jnp.sum(got[...], axis=0)
    for k in range(1, hidden_count):
        pltpu.make_async_remote_copy(
            tile, tiles.at[hid], tail_send.at[1], tail_recv.at[1],
            device_id=(dp, lax.rem(hid + k, hidden_count)), device_id_type=MESH,
        ).start()
    wait(tiles.at[pl.ds(0, hidden_count - 1)], tail_recv.at[1])
    tiles[hid] = tile[...]
    total = jnp.sum(tiles[...], axis=0)
    query = lax.broadcasted_iota(jnp.int32, (8, 128), 0) + 2 * hid
    pick = (lax.broadcasted_iota(jnp.int32, (8, 128), 1) == query).astype(jnp.float32)
    result = lax.dot_general(
        pick, total, NT, precision=lax.Precision.HIGHEST, preferred_element_type=jnp.float32
    )
    out[...] = result[:2]

    wait(tok.at[pl.ds(0, 7 * 16)], z_send)
    wait(tok.at[pl.ds(0, 7 * 48)], x_send)
    wait(tok.at[pl.ds(0, 7 * 64)], c_send.at[0])
    wait(rb.at[:, pl.ds(0, 256)], c_send.at[1])
    wait(sb.at[:, pl.ds(0, 4)], c_send.at[2])
    wait(wb.at[pl.ds(0, 7)], w_send)
    wait(wb.at[pl.ds(0, 24)], y_send)
    wait(rb.at[pl.ds(0, 7), pl.ds(0, 64)], r_send.at[0])
    wait(sb.at[pl.ds(0, 7), pl.ds(0, 1)], r_send.at[1])
    wait(idb.at[pl.ds(0, 7)], r_send.at[2])
    wait(rb.at[:, pl.ds(0, 128)], r_send.at[3])
    wait(sb.at[:, pl.ds(0, 2)], r_send.at[4])
    wait(rb.at[:, pl.ds(0, 64)], r_send.at[5])
    wait(sb.at[:, pl.ds(0, 1)], r_send.at[6])
    wait(got.at[pl.ds(0, 31)], tail_send.at[0])
    wait(tiles.at[pl.ds(0, hidden_count - 1)], tail_send.at[1])


def local(tokens, gate_weight, up_weight, cotangent, query_left, query_right, doc_ids, doc_slot):
    bf16, f32, i32 = jnp.bfloat16, jnp.float32, jnp.int32
    dma = pltpu.SemaphoreType.DMA
    anywhere = pl.BlockSpec(memory_space=pltpu.HBM)
    return pl.pallas_call(
        kernel,
        out_shape=jax.ShapeDtypeStruct((2, 8), f32),
        in_specs=[anywhere] * 8,
        out_specs=pl.BlockSpec(memory_space=pltpu.VMEM),
        scratch_shapes=[
            pltpu.VMEM((1024, 4096), bf16),
            pltpu.VMEM((32, 2 * F, 128), bf16),
            pltpu.VMEM((8, 512, 128), jnp.int16),
            pltpu.VMEM((8, 8, 1, 128), f32),
            pltpu.VMEM((8, 1, 128), i32),
            pltpu.VMEM((128, 1792), bf16),
            pltpu.VMEM((128, 1792), bf16),
            pltpu.VMEM((1792, 128), bf16),
            pltpu.VMEM((1792, 128), bf16),
            pltpu.VMEM((128, 4096), bf16),
            pltpu.VMEM((64, 4096), bf16),
            pltpu.VMEM((512, 384), bf16),
            pltpu.VMEM((1, 128), i32),
            pltpu.VMEM((1, 256), i32),
            pltpu.VMEM((2 * F, 256), f32),
            pltpu.VMEM((384, 256), bf16),
            pltpu.VMEM((128, 1024), f32),
            pltpu.VMEM((256, 1024), bf16),
            pltpu.VMEM((32, 8, 128), f32),
            pltpu.VMEM((32, 8, 128), f32),
            pltpu.VMEM((8, 128), f32),
            pltpu.VMEM((8, 8, 128), f32),
            dma((8,)), dma, dma, dma((3,)), dma, dma, dma((7,)), dma((2,)),
            dma((9,)), dma((8, 2)), dma((8, 2)), dma((8,)), dma((8,)), dma((8, 2)), dma((8, 2)),
            dma((3, 8)), dma((2, 5, 2)), dma((3, 5)), dma((2, 5)), dma((2,)),
        ],
        compiler_params=pltpu.CompilerParams(
            collective_id=0, has_side_effects=True, vmem_limit_bytes=60 * 1024 * 1024
        ),
        name="influence",
    )(
        tokens, gate_weight, up_weight, cotangent, query_left, query_right,
        doc_ids.reshape(1, -1), doc_slot.reshape(1, -1),
    )


def solution(mesh):
    return jax.shard_map(
        local,
        mesh=mesh,
        in_specs=(
            P("dp", None),
            P("dp", "hidden"),
            P("dp", "hidden"),
            P("dp", None),
            P(None, "hidden"),
            P("hidden", None),
            P("dp"),
            P(),
        ),
        out_specs=P("hidden", "dp"),
        check_vma=False,
    )
```

```python
import jax
import jax.numpy as jnp
from jax import lax
from jax.experimental import pallas as pl
from jax.experimental.pallas import tpu as pltpu
from jax.sharding import PartitionSpec as P

MESH = pl.DeviceIdType.MESH
NT = (((1,), (1,)), ((), ()))
NX, NY, NZ = 4, 4, 8
R = 32
F = 224
DIST = (0, -1, 1, -2, 2, -3, 3, 4)
PLACE = {d: i for i, d in enumerate(DIST)}
PLACE[-4] = PLACE[4]


def kernel(
    tokens, gate, up, cot, ql, qr, ids, slot, out,
    tok, wb, rb, sb, idb, gate_v, up_v, gate_t, up_t, cot_v, qr_v, ql_v, ids_v, slot_v,
    acc, act, scores, spread, part, got, tile, tiles,
    local_sem, z_send, x_send, c_send, w_send, y_send, r_send, tail_send,
    z_recv, x_recv, xh_recv, c_recv, w_recv, y_recv, yh_recv,
    rz_recv, rx_recv, rxh_recv, rc_recv, tail_recv,
):
    dp, hid = lax.axis_index("dp"), lax.axis_index("hidden")
    y, z = dp // NZ, lax.rem(dp, NZ)
    x, c = hid // 2, lax.rem(hid, 2)
    hidden_count = 2 * NX

    def at(dx=0, dy=0, dz=0, dc=0):
        return (
            lax.rem(y + dy + NY, NY) * NZ + lax.rem(z + dz + NZ, NZ),
            lax.rem(x + dx + NX, NX) * 2 + lax.rem(c + dc, 2),
        )

    def send(src, dst, send_sem, recv_sem, **where):
        pltpu.make_async_remote_copy(
            src, dst, send_sem, recv_sem, device_id=at(**where), device_id_type=MESH
        ).start()

    def wait(ref, sem):
        pltpu.make_async_copy(ref, ref, sem).wait()

    loads = [
        pltpu.make_async_copy(gate, gate_v, local_sem.at[0]),
        pltpu.make_async_copy(up, up_v, local_sem.at[1]),
        pltpu.make_async_copy(cot, cot_v, local_sem.at[2]),
        pltpu.make_async_copy(qr, qr_v, local_sem.at[3]),
        pltpu.make_async_copy(ids, ids_v, local_sem.at[4]),
        pltpu.make_async_copy(slot, slot_v, local_sem.at[5]),
        pltpu.make_async_copy(
            ql.at[:, pl.ds(pl.multiple_of((5 * z) // 3 * 128, 128), 384)], ql_v, local_sem.at[6]
        ),
        pltpu.make_async_copy(tokens, tok.at[pl.ds(0, 128)], local_sem.at[7]),
    ]
    for load in loads:
        load.start()

    barrier = pltpu.get_barrier_semaphore()
    peers = [dict(dz=1), dict(dz=-1), dict(dx=1), dict(dx=-1), dict(dy=1), dict(dy=-1), dict(dc=1)]
    for peer in peers:
        pl.semaphore_signal(barrier, inc=1, device_id=at(**peer), device_id_type=MESH)
    pl.semaphore_wait(barrier, len(peers))

    def rows(d, dx=0):
        first = c * 64 + lax.rem(x + dx + NX, NX) * 16
        return pl.ds(pl.multiple_of(PLACE[d] * 128 + first, 16), 16)

    half = (pl.ds(0, 2048), pl.ds(2048, 2048))
    own_rows = pl.ds(pl.multiple_of(c * 64 + x * 16, 16), 16)
    for i in range(2):
        for s in (1, -1):
            send(
                tokens.at[own_rows, half[i]], tok.at[rows(-s), half[i]], z_send,
                z_recv.at[PLACE[-s], i], dz=s,
            )

    loads[2].wait()
    loads[3].wait()

    def k_rows(dx=0, first=0, count=64):
        start = c * 256 + lax.rem(x + dx + NX, NX) * 64 + first
        return pl.ds(pl.multiple_of(start, count), count)

    def scale_row(dx=0):
        return pl.ds(c * 4 + lax.rem(x + dx + NX, NX), 1)

    right = lax.dot_general(qr_v[...], cot_v[...], NT, preferred_element_type=jnp.float32)
    largest = jnp.maximum(jnp.max(jnp.abs(right), axis=0, keepdims=True), 1e-30)
    steps = right * (32000.0 / largest)
    steps = steps + jnp.where(steps >= 0, 0.5, -0.5)
    rb[0, k_rows(), :] = steps.astype(jnp.int32).astype(jnp.int16)
    sb[0, c * 4 + x] = largest / 32000.0
    loads[4].wait()
    idb[0] = ids_v[...]

    def right_along_z(d, s):
        to = PLACE[d - s]
        here = PLACE[d]
        send(rb.at[here, k_rows()], rb.at[to, k_rows()], r_send.at[0], rz_recv.at[0, to], dz=s)
        send(sb.at[here, scale_row()], sb.at[to, scale_row()], r_send.at[1], rz_recv.at[1, to], dz=s)
        send(idb.at[here], idb.at[to], r_send.at[2], rz_recv.at[2, to], dz=s)

    def group(g):
        return (0,) if g == 0 else (4,) if g == 4 else (-g, g)

    def places(g):
        return pl.ds(PLACE[group(g)[0]], len(group(g)))

    def right_along_x(g):
        for s in (1, -1):
            i = (1 - s) // 2
            mine = rb.at[places(g), k_rows()]
            send(mine, mine, r_send.at[3], rx_recv.at[0, g, i], dx=s)
            mine = sb.at[places(g), scale_row()]
            send(mine, mine, r_send.at[4], rx_recv.at[1, g, i], dx=s)

    def pass_right(g):
        for s in (1, -1):
            i = (1 - s) // 2
            wait(rb.at[places(g), k_rows(-s)], rx_recv.at[0, g, i])
            wait(sb.at[places(g), scale_row(-s)], rx_recv.at[1, g, i])
            piece = rb.at[places(g), k_rows(-s, 32 * i, 32)]
            send(piece, piece, r_send.at[5], rxh_recv.at[i, g], dx=s)
        piece = sb.at[places(g), scale_row(-1)]
        send(piece, piece, r_send.at[6], rxh_recv.at[2, g], dx=1)

    def swap_right(g):
        for i in range(2):
            wait(rb.at[places(g), k_rows(2, 32 * i, 32)], rxh_recv.at[i, g])
        wait(sb.at[places(g), scale_row(2)], rxh_recv.at[2, g])
        mine = rb.at[places(g), pl.ds(pl.multiple_of(c * 256, 256), 256)]
        send(mine, mine, c_send.at[1], rc_recv.at[0, g], dc=1)
        mine = sb.at[places(g), pl.ds(c * 4, 4)]
        send(mine, mine, c_send.at[2], rc_recv.at[1, g], dc=1)

    for s in (1, -1):
        right_along_z(0, s)

    loads[0].wait()
    loads[1].wait()

    @pl.loop(0, 14)
    def _(i):
        at_tile = pl.ds(pl.multiple_of(i * 128, 128), 128)
        gate_t[at_tile, :] = gate_v[:, at_tile].T
        up_t[at_tile, :] = up_v[:, at_tile].T

    def window(dz=0, dy=0):
        return lax.rem(y + dy + NY, NY) * NZ + lax.rem(z + dz + NZ, NZ)

    def units(dz):
        return pl.ds(pl.multiple_of(lax.rem(z + dz + NZ, NZ) * F, 32), F)

    upper, lower = pl.ds(0, F), pl.ds(F, F)

    def exchange_weights(d):
        send(gate_t.at[units(d)], wb.at[dp, upper], w_send, w_recv.at[PLACE[-d], 0], dz=d)
        send(up_t.at[units(d)], wb.at[dp, lower], w_send, w_recv.at[PLACE[-d], 1], dz=d)

    def order(s):
        return (0, 1) if s == 1 else (1, 0)

    parts = (upper, lower)
    for s in (1, -1):
        for i in order(s):
            piece = (gate_t, up_t)[i].at[units(0)]
            send(piece, wb.at[dp, parts[i]], y_send, y_recv.at[0, (1 - s) // 2, i], dy=s)
    for d in (1, -1):
        exchange_weights(d)
    wb[dp, upper, :] = gate_t[units(0), :]
    wb[dp, lower, :] = up_t[units(0), :]

    def tokens_along_x(d, i):
        piece = tok.at[rows(d), half[i]]
        for s in (1, -1):
            send(piece, piece, x_send, x_recv.at[PLACE[d], (1 - s) // 2, i], dx=s)

    def to_core(d, dx):
        piece = tok.at[rows(d, dx)]
        send(piece, piece, c_send.at[0], c_recv.at[PLACE[d]], dc=1)

    def pass_tokens(d):
        for s in (1, -1):
            i = (1 - s) // 2
            wait(tok.at[rows(d), half[i]], x_recv.at[PLACE[d], i, i])
            piece = tok.at[rows(d, -s), half[i]]
            send(piece, piece, x_send, xh_recv.at[PLACE[d], i], dx=s)
        for s in (1, -1):
            i = (1 - s) // 2
            wait(tok.at[rows(d), half[i]], x_recv.at[PLACE[d], i, 1 - i])
            to_core(d, -s)

    def swap_cores(d):
        for i in range(2):
            wait(tok.at[rows(d), half[i]], xh_recv.at[PLACE[d], i])
        to_core(d, 2)

    def weights_along_y(d, i):
        piece = wb.at[window(d), parts[i]]
        for s in (1, -1):
            send(piece, piece, y_send, y_recv.at[PLACE[d], (1 - s) // 2, i], dy=s)

    def pass_weights(d):
        for s in (1, -1):
            i = (1 - s) // 2
            wait(wb.at[dp, upper], y_recv.at[PLACE[d], i, i])
            piece = wb.at[window(d, -s), parts[i]]
            send(piece, piece, y_send, yh_recv.at[PLACE[d], i], dy=s)

    def alone(group):
        return isinstance(group, int) and group in (0, 4)

    def token_span(group):
        if alone(group):
            return pl.ds(7 * 128 * (group // 4), 128)
        return pl.ds(pl.multiple_of(256 * group - 128, 128), 256)

    def spread_documents():
        loads[5].wait()
        columns = lax.broadcasted_iota(jnp.int32, (256, 256), 0)
        placing = (columns == slot_v[...]).astype(jnp.float32).astype(jnp.bfloat16)
        docs = lax.broadcasted_iota(jnp.int32, (256, 128), 0)
        for place in range(NZ):
            one_hot = (docs == idb[place]).astype(jnp.float32).astype(jnp.bfloat16)
            spread[:, pl.ds(place * 128, 128)] = jnp.dot(
                placing, one_hot, preferred_element_type=jnp.float32
            ).astype(jnp.bfloat16)

    def multiply(pair, first, count):
        blocks = [lax.rem(z + distance + NZ, NZ) for distance in (pair, -1 - pair)]
        blocks = [i * NZ + block for block in blocks for i in range(NY)]
        span = pl.ds(first, count)
        weights = jnp.concatenate([wb[block] for block in blocks], axis=1)
        lanes = [pl.ds(pl.multiple_of(block * 128, 128), 128) for block in blocks]
        inputs = jnp.concatenate([tok[span, lane] for lane in lanes], axis=1)
        acc[:, span] += lax.dot_general(weights, inputs, NT, preferred_element_type=jnp.float32)

    def await_tokens(g):
        for d in group(g):
            wait(tok.at[pl.ds(0, 64)], c_recv.at[PLACE[d]])

    def await_weights(g):
        for d in group(g):
            for i in range(2):
                wait(wb.at[dp, upper], y_recv.at[PLACE[d], i, 1 - i])
                wait(wb.at[dp, upper], yh_recv.at[PLACE[d], i])

    def finish(group):
        span = token_span(group)
        first_place = 7 * (group // 4) if alone(group) else 2 * group - 1
        count = 1 if alone(group) else 2
        gates = acc[:F, span]
        act[pl.ds(first, F), span] = (gates / (1.0 + jnp.exp(-gates)) * acc[F:, span]).astype(jnp.bfloat16)
        left = jnp.dot(ql_v[...], act[:, span], preferred_element_type=jnp.float32)
        for q in range(16):
            hidden = q // 2
            at_row = hidden % 2 * 256 + hidden // 2 * 64 + q % 2 * R
            right = [
                rb[first_place + i, at_row:at_row + R].astype(jnp.int32).astype(jnp.float32)
                * sb[first_place + i, hidden % 2 * 4 + hidden // 2]
                for i in range(count)
            ]
            right = right[0] if count == 1 else jnp.concatenate(right, axis=1)
            scores[q:q + 1, span] = jnp.sum(
                left[q * R:(q + 1) * R] * right, axis=0, keepdims=True
            )

    right_along_x(0)
    acc[...] = jnp.zeros_like(acc)
    act[...] = jnp.zeros_like(act)
    scores[...] = jnp.zeros_like(scores)
    first = pl.multiple_of(F * z - (5 * z) // 3 * 128, 32)
    for g in range(1, 5):
        if g < 4:
            for i in range(2):
                for d in group(g):
                    s = 1 if d < 0 else -1
                    place = PLACE[d]
                    wait(tok.at[rows(d), half[i]], z_recv.at[place, i])
                    if g < 3 or s == 1 - 2 * i:
                        piece = tok.at[rows(d), half[i]]
                        send(piece, tok.at[rows(d - s), half[i]], z_send, z_recv.at[PLACE[d - s], i], dz=s)
                    tokens_along_x(d, i)
        else:
            for i in range(2):
                wait(tok.at[rows(4), half[i]], z_recv.at[PLACE[4], i])
                tokens_along_x(4, i)
        for d in group(g):
            to_core(d, 0)
        for d in group(g):
            for i in range(3):
                wait((rb.at[0, k_rows()], sb.at[0, scale_row()], idb.at[0])[i], rz_recv.at[i, PLACE[d]])
            s = 1 if d < 0 else -1
            if g < 3 or d == -3:
                right_along_z(d, s)
        right_along_x(g)
        for d in group(g + 1) if g < 4 else ():
            exchange_weights(d)
        if g > 1:
            for d in group(g - 1):
                pass_tokens(d)
            pass_right(g - 1)
        if g > 2:
            for d in group(g - 2):
                swap_cores(d)
            swap_right(g - 2)
        for d in group(g - 1):
            pass_weights(d)
        if g == 1:
            pass_right(0)
        if g == 3:
            loads[7].wait()
            await_weights(0)
            await_weights(1)
            await_tokens(1)
            multiply(0, 0, 384)
        if g == 4:
            spread_documents()
            await_weights(2)
            multiply(1, 0, 384)
        for i in range(2):
            for d in group(g):
                wait(wb.at[dp, upper], w_recv.at[PLACE[d], i])
                weights_along_y(d, i)
        if g == 2:
            swap_right(0)
    pass_tokens(4)
    pass_right(4)
    for d in group(3):
        swap_cores(d)
    swap_right(3)
    await_tokens(2)
    pl.loop(0, 2)(lambda pair: multiply(pair, 384, 256))
    pass_weights(4)
    swap_cores(4)
    swap_right(4)
    await_weights(3)
    multiply(2, 0, 640)
    await_tokens(3)
    pl.loop(0, 3)(lambda pair: multiply(pair, 640, 256))
    for g in range(5):
        wait(rb.at[places(g), pl.ds(0, 256)], rc_recv.at[0, g])
        wait(sb.at[places(g), pl.ds(0, 4)], rc_recv.at[1, g])
    loads[6].wait()
    await_weights(4)
    multiply(3, 0, 896)
    finish(0)
    pl.loop(1, 4)(finish)
    await_tokens(4)
    weights = jnp.concatenate([wb[i] for i in range(NY * NZ)], axis=1)
    acc[:, 896:] = lax.dot_general(weights, tok[896:, :], NT, preferred_element_type=jnp.float32)
    finish(4)

    rest = scores[...]
    columns_sum = jnp.zeros((256, 128), jnp.float32)
    for _ in range(3):
        rounded = rest.astype(jnp.bfloat16)
        rest = rest - rounded.astype(jnp.float32)
        columns_sum += lax.dot_general(spread[...], rounded, NT, preferred_element_type=jnp.float32)
    part[...] = columns_sum.reshape(32, 8, 128)

    @pl.loop(1, 32)
    def _(k):
        to = lax.rem(dp + k, 32)
        pltpu.make_async_remote_copy(
            part.at[to], got.at[dp], tail_send.at[0], tail_recv.at[0],
            device_id=(to, hid), device_id_type=MESH,
        ).start()

    wait(got.at[pl.ds(0, 31)], tail_recv.at[0])
    got[dp] = part[dp]
    tile[...] = jnp.sum(got[...], axis=0)
    for k in range(1, hidden_count):
        pltpu.make_async_remote_copy(
            tile, tiles.at[hid], tail_send.at[1], tail_recv.at[1],
            device_id=(dp, lax.rem(hid + k, hidden_count)), device_id_type=MESH,
        ).start()
    wait(tiles.at[pl.ds(0, hidden_count - 1)], tail_recv.at[1])
    tiles[hid] = tile[...]
    total = jnp.sum(tiles[...], axis=0)
    query = lax.broadcasted_iota(jnp.int32, (8, 128), 0) + 2 * hid
    pick = (lax.broadcasted_iota(jnp.int32, (8, 128), 1) == query).astype(jnp.float32)
    result = lax.dot_general(
        pick, total, NT, precision=lax.Precision.HIGHEST, preferred_element_type=jnp.float32
    )
    out[...] = result[:2]

    wait(tok.at[pl.ds(0, 7 * 16)], z_send)
    wait(tok.at[pl.ds(0, 7 * 48)], x_send)
    wait(tok.at[pl.ds(0, 7 * 64)], c_send.at[0])
    wait(rb.at[:, pl.ds(0, 256)], c_send.at[1])
    wait(sb.at[:, pl.ds(0, 4)], c_send.at[2])
    wait(wb.at[pl.ds(0, 7)], w_send)
    wait(wb.at[pl.ds(0, 24)], y_send)
    wait(rb.at[pl.ds(0, 7), pl.ds(0, 64)], r_send.at[0])
    wait(sb.at[pl.ds(0, 7), pl.ds(0, 1)], r_send.at[1])
    wait(idb.at[pl.ds(0, 7)], r_send.at[2])
    wait(rb.at[:, pl.ds(0, 128)], r_send.at[3])
    wait(sb.at[:, pl.ds(0, 2)], r_send.at[4])
    wait(rb.at[:, pl.ds(0, 64)], r_send.at[5])
    wait(sb.at[:, pl.ds(0, 1)], r_send.at[6])
    wait(got.at[pl.ds(0, 31)], tail_send.at[0])
    wait(tiles.at[pl.ds(0, hidden_count - 1)], tail_send.at[1])


def local(tokens, gate_weight, up_weight, cotangent, query_left, query_right, doc_ids, doc_slot):
    bf16, f32, i32 = jnp.bfloat16, jnp.float32, jnp.int32
    dma = pltpu.SemaphoreType.DMA
    anywhere = pl.BlockSpec(memory_space=pltpu.HBM)
    return pl.pallas_call(
        kernel,
        out_shape=jax.ShapeDtypeStruct((2, 8), f32),
        in_specs=[anywhere] * 8,
        out_specs=pl.BlockSpec(memory_space=pltpu.VMEM),
        scratch_shapes=[
            pltpu.VMEM((1024, 4096), bf16),
            pltpu.VMEM((32, 2 * F, 128), bf16),
            pltpu.VMEM((8, 512, 128), jnp.int16),
            pltpu.VMEM((8, 8, 1, 128), f32),
            pltpu.VMEM((8, 1, 128), i32),
            pltpu.VMEM((128, 1792), bf16),
            pltpu.VMEM((128, 1792), bf16),
            pltpu.VMEM((1792, 128), bf16),
            pltpu.VMEM((1792, 128), bf16),
            pltpu.VMEM((128, 4096), bf16),
            pltpu.VMEM((64, 4096), bf16),
            pltpu.VMEM((512, 384), bf16),
            pltpu.VMEM((1, 128), i32),
            pltpu.VMEM((1, 256), i32),
            pltpu.VMEM((2 * F, 1024), f32),
            pltpu.VMEM((384, 1024), bf16),
            pltpu.VMEM((128, 1024), f32),
            pltpu.VMEM((256, 1024), bf16),
            pltpu.VMEM((32, 8, 128), f32),
            pltpu.VMEM((32, 8, 128), f32),
            pltpu.VMEM((8, 128), f32),
            pltpu.VMEM((8, 8, 128), f32),
            dma((8,)), dma, dma, dma((3,)), dma, dma, dma((7,)), dma((2,)),
            dma((8, 2)), dma((8, 2, 2)), dma((8, 2)), dma((8,)), dma((8, 2)), dma((8, 2, 2)), dma((8, 2)),
            dma((3, 8)), dma((2, 5, 2)), dma((3, 5)), dma((2, 5)), dma((2,)),
        ],
        compiler_params=pltpu.CompilerParams(
            collective_id=0, has_side_effects=True, vmem_limit_bytes=60 * 1024 * 1024
        ),
        name="influence",
    )(
        tokens, gate_weight, up_weight, cotangent, query_left, query_right,
        doc_ids.reshape(1, -1), doc_slot.reshape(1, -1),
    )


def solution(mesh):
    return jax.shard_map(
        local,
        mesh=mesh,
        in_specs=(
            P("dp", None),
            P("dp", "hidden"),
            P("dp", "hidden"),
            P("dp", None),
            P(None, "hidden"),
            P("hidden", None),
            P("dp"),
            P(),
        ),
        out_specs=P("hidden", "dp"),
        check_vma=False,
    )
```

```python
import jax
import jax.numpy as jnp
from jax import lax
from jax.experimental import pallas as pl
from jax.experimental.pallas import tpu as pltpu
from jax.sharding import PartitionSpec as P

MESH = pl.DeviceIdType.MESH
NT = (((1,), (1,)), ((), ()))
NX, NY, NZ = 4, 4, 8
R = 32
F = 224
DIST = (0, -1, 1, -2, 2, -3, 3, 4)
PLACE = {d: i for i, d in enumerate(DIST)}
PLACE[-4] = PLACE[4]


def kernel(
    tokens, gate, up, cot, ql, qr, ids, slot, out,
    tok, wb, rb, sb, idb, gate_v, up_v, gate_t, up_t, cot_v, qr_v, ql_v, ids_v, slot_v,
    acc, act, scores, spread, part, got, tile, tiles,
    local_sem, z_send, x_send, c_send, w_send, y_send, r_send, tail_send,
    z_recv, x_recv, xh_recv, c_recv, w_recv, y_recv, yh_recv,
    rz_recv, rx_recv, rxh_recv, rc_recv, tail_recv,
):
    dp, hid = lax.axis_index("dp"), lax.axis_index("hidden")
    y, z = dp // NZ, lax.rem(dp, NZ)
    x, c = hid // 2, lax.rem(hid, 2)
    hidden_count = 2 * NX

    def at(dx=0, dy=0, dz=0, dc=0):
        return (
            lax.rem(y + dy + NY, NY) * NZ + lax.rem(z + dz + NZ, NZ),
            lax.rem(x + dx + NX, NX) * 2 + lax.rem(c + dc, 2),
        )

    def send(src, dst, send_sem, recv_sem, **where):
        pltpu.make_async_remote_copy(
            src, dst, send_sem, recv_sem, device_id=at(**where), device_id_type=MESH
        ).start()

    def wait(ref, sem):
        pltpu.make_async_copy(ref, ref, sem).wait()

    loads = [
        pltpu.make_async_copy(gate, gate_v, local_sem.at[0]),
        pltpu.make_async_copy(up, up_v, local_sem.at[1]),
        pltpu.make_async_copy(cot, cot_v, local_sem.at[2]),
        pltpu.make_async_copy(qr, qr_v, local_sem.at[3]),
        pltpu.make_async_copy(ids, ids_v, local_sem.at[4]),
        pltpu.make_async_copy(slot, slot_v, local_sem.at[5]),
        pltpu.make_async_copy(
            ql.at[:, pl.ds(pl.multiple_of((5 * z) // 3 * 128, 128), 384)], ql_v, local_sem.at[6]
        ),
        pltpu.make_async_copy(tokens, tok.at[pl.ds(0, 128)], local_sem.at[7]),
    ]
    for load in loads:
        load.start()

    barrier = pltpu.get_barrier_semaphore()
    peers = [dict(dz=1), dict(dz=-1), dict(dx=1), dict(dx=-1), dict(dy=1), dict(dy=-1), dict(dc=1)]
    for peer in peers:
        pl.semaphore_signal(barrier, inc=1, device_id=at(**peer), device_id_type=MESH)
    pl.semaphore_wait(barrier, len(peers))

    def rows(d, dx=0):
        first = c * 64 + lax.rem(x + dx + NX, NX) * 16
        return pl.ds(pl.multiple_of(PLACE[d] * 128 + first, 16), 16)

    half = (pl.ds(0, 2048), pl.ds(2048, 2048))
    own_rows = pl.ds(pl.multiple_of(c * 64 + x * 16, 16), 16)
    for i in range(2):
        for s in (1, -1):
            send(
                tokens.at[own_rows, half[i]], tok.at[rows(-s), half[i]], z_send,
                z_recv.at[PLACE[-s], i], dz=s,
            )

    loads[2].wait()
    loads[3].wait()

    def k_rows(dx=0, first=0, count=64):
        start = c * 256 + lax.rem(x + dx + NX, NX) * 64 + first
        return pl.ds(pl.multiple_of(start, count), count)

    def scale_row(dx=0):
        return pl.ds(c * 4 + lax.rem(x + dx + NX, NX), 1)

    right = lax.dot_general(qr_v[...], cot_v[...], NT, preferred_element_type=jnp.float32)
    largest = jnp.maximum(jnp.max(jnp.abs(right), axis=0, keepdims=True), 1e-30)
    steps = right * (32000.0 / largest)
    steps = steps + jnp.where(steps >= 0, 0.5, -0.5)
    rb[0, k_rows(), :] = steps.astype(jnp.int32).astype(jnp.int16)
    sb[0, c * 4 + x] = largest / 32000.0
    loads[4].wait()
    idb[0] = ids_v[...]

    def right_along_z(d, s):
        to = PLACE[d - s]
        here = PLACE[d]
        send(rb.at[here, k_rows()], rb.at[to, k_rows()], r_send.at[0], rz_recv.at[0, to], dz=s)
        send(sb.at[here, scale_row()], sb.at[to, scale_row()], r_send.at[1], rz_recv.at[1, to], dz=s)
        send(idb.at[here], idb.at[to], r_send.at[2], rz_recv.at[2, to], dz=s)

    def group(g):
        return (0,) if g == 0 else (4,) if g == 4 else (-g, g)

    def places(g):
        return pl.ds(PLACE[group(g)[0]], len(group(g)))

    def right_along_x(g):
        for s in (1, -1):
            i = (1 - s) // 2
            mine = rb.at[places(g), k_rows()]
            send(mine, mine, r_send.at[3], rx_recv.at[0, g, i], dx=s)
            mine = sb.at[places(g), scale_row()]
            send(mine, mine, r_send.at[4], rx_recv.at[1, g, i], dx=s)

    def pass_right(g):
        for s in (1, -1):
            i = (1 - s) // 2
            wait(rb.at[places(g), k_rows(-s)], rx_recv.at[0, g, i])
            wait(sb.at[places(g), scale_row(-s)], rx_recv.at[1, g, i])
            piece = rb.at[places(g), k_rows(-s, 32 * i, 32)]
            send(piece, piece, r_send.at[5], rxh_recv.at[i, g], dx=s)
        piece = sb.at[places(g), scale_row(-1)]
        send(piece, piece, r_send.at[6], rxh_recv.at[2, g], dx=1)

    def swap_right(g):
        for i in range(2):
            wait(rb.at[places(g), k_rows(2, 32 * i, 32)], rxh_recv.at[i, g])
        wait(sb.at[places(g), scale_row(2)], rxh_recv.at[2, g])
        mine = rb.at[places(g), pl.ds(pl.multiple_of(c * 256, 256), 256)]
        send(mine, mine, c_send.at[1], rc_recv.at[0, g], dc=1)
        mine = sb.at[places(g), pl.ds(c * 4, 4)]
        send(mine, mine, c_send.at[2], rc_recv.at[1, g], dc=1)

    for s in (1, -1):
        right_along_z(0, s)

    loads[0].wait()
    loads[1].wait()

    @pl.loop(0, 14)
    def _(i):
        at_tile = pl.ds(pl.multiple_of(i * 128, 128), 128)
        gate_t[at_tile, :] = gate_v[:, at_tile].T
        up_t[at_tile, :] = up_v[:, at_tile].T

    def window(dz=0, dy=0):
        return lax.rem(y + dy + NY, NY) * NZ + lax.rem(z + dz + NZ, NZ)

    def units(dz):
        return pl.ds(pl.multiple_of(lax.rem(z + dz + NZ, NZ) * F, 32), F)

    upper, lower = pl.ds(0, F), pl.ds(F, F)

    def exchange_weights(d):
        send(gate_t.at[units(d)], wb.at[dp, upper], w_send, w_recv.at[PLACE[-d], 0], dz=d)
        send(up_t.at[units(d)], wb.at[dp, lower], w_send, w_recv.at[PLACE[-d], 1], dz=d)

    def order(s):
        return (0, 1) if s == 1 else (1, 0)

    parts = (upper, lower)
    for s in (1, -1):
        for i in order(s):
            piece = (gate_t, up_t)[i].at[units(0)]
            send(piece, wb.at[dp, parts[i]], y_send, y_recv.at[0, (1 - s) // 2, i], dy=s)
    for d in (1, -1):
        exchange_weights(d)
    wb[dp, upper, :] = gate_t[units(0), :]
    wb[dp, lower, :] = up_t[units(0), :]

    def tokens_along_x(d, i):
        piece = tok.at[rows(d), half[i]]
        for s in (1, -1):
            send(piece, piece, x_send, x_recv.at[PLACE[d], (1 - s) // 2, i], dx=s)

    def to_core(d, dx):
        piece = tok.at[rows(d, dx)]
        send(piece, piece, c_send.at[0], c_recv.at[PLACE[d]], dc=1)

    def pass_tokens(d):
        for s in (1, -1):
            i = (1 - s) // 2
            wait(tok.at[rows(d), half[i]], x_recv.at[PLACE[d], i, i])
            piece = tok.at[rows(d, -s), half[i]]
            send(piece, piece, x_send, xh_recv.at[PLACE[d], i], dx=s)
        for s in (1, -1):
            i = (1 - s) // 2
            wait(tok.at[rows(d), half[i]], x_recv.at[PLACE[d], i, 1 - i])
            to_core(d, -s)

    def swap_cores(d):
        for i in range(2):
            wait(tok.at[rows(d), half[i]], xh_recv.at[PLACE[d], i])
        to_core(d, 2)

    def weights_along_y(d, i):
        piece = wb.at[window(d), parts[i]]
        for s in (1, -1):
            send(piece, piece, y_send, y_recv.at[PLACE[d], (1 - s) // 2, i], dy=s)

    def pass_weights(d):
        for s in (1, -1):
            i = (1 - s) // 2
            wait(wb.at[dp, upper], y_recv.at[PLACE[d], i, i])
            piece = wb.at[window(d, -s), parts[i]]
            send(piece, piece, y_send, yh_recv.at[PLACE[d], i], dy=s)

    def spread_documents():
        loads[5].wait()
        row = lax.broadcasted_iota(jnp.int32, (256, 256), 0)
        columns = (row & 31) * 8 + lax.shift_right_logical(row, 5)
        placing = (columns == slot_v[...]).astype(jnp.float32).astype(jnp.bfloat16)
        docs = lax.broadcasted_iota(jnp.int32, (256, 128), 0)
        for place in range(NZ):
            one_hot = (docs == idb[place]).astype(jnp.float32).astype(jnp.bfloat16)
            spread[:, pl.ds(place * 128, 128)] = jnp.dot(
                placing, one_hot, preferred_element_type=jnp.float32
            ).astype(jnp.bfloat16)

    def multiply(taken, first, count):
        blocks = [lax.rem(z + DIST[place] + NZ, NZ) for place in taken]
        blocks = [i * NZ + block for block in blocks for i in range(NY)]
        span = pl.ds(first, count)
        weights = jnp.concatenate([wb[block] for block in blocks], axis=1)
        lanes = [pl.ds(pl.multiple_of(block * 128, 128), 128) for block in blocks]
        inputs = jnp.concatenate([tok[span, lane] for lane in lanes], axis=1)
        product = lax.dot_general(weights, inputs, NT, preferred_element_type=jnp.float32)
        acc[:, span] = product if 0 in taken else acc[:, span] + product

    def await_tokens(g):
        for d in group(g):
            wait(tok.at[pl.ds(0, 64)], c_recv.at[PLACE[d]])

    def await_weights(g):
        for d in group(g):
            for i in range(2):
                wait(wb.at[dp, upper], y_recv.at[PLACE[d], i, 1 - i])
                wait(wb.at[dp, upper], yh_recv.at[PLACE[d], i])

    def finish(j):
        span = pl.ds(j * 256, 256)
        gates = acc[:F, span]
        act[pl.ds(first, F), span] = (gates / (1.0 + jnp.exp(-gates)) * acc[F:, span]).astype(jnp.bfloat16)
        left = jnp.dot(ql_v[...], act[:, span], preferred_element_type=jnp.float32)
        for q in range(16):
            hidden = q // 2
            at_row = hidden % 2 * 256 + hidden // 2 * 64 + q % 2 * R
            right = [
                rb[2 * j + i, at_row:at_row + R].astype(jnp.int32).astype(jnp.float32)
                * sb[2 * j + i, hidden % 2 * 4 + hidden // 2]
                for i in range(2)
            ]
            scores[q:q + 1, span] = jnp.sum(
                left[q * R:(q + 1) * R] * jnp.concatenate(right, axis=1), axis=0, keepdims=True
            )

    right_along_x(0)
    act[...] = jnp.zeros_like(act)
    scores[...] = jnp.zeros_like(scores)
    first = pl.multiple_of(F * z - (5 * z) // 3 * 128, 32)
    for g in range(1, 5):
        if g < 4:
            for i in range(2):
                for d in group(g):
                    s = 1 if d < 0 else -1
                    place = PLACE[d]
                    wait(tok.at[rows(d), half[i]], z_recv.at[place, i])
                    if g < 3 or s == 1 - 2 * i:
                        piece = tok.at[rows(d), half[i]]
                        send(piece, tok.at[rows(d - s), half[i]], z_send, z_recv.at[PLACE[d - s], i], dz=s)
                    tokens_along_x(d, i)
        else:
            for i in range(2):
                wait(tok.at[rows(4), half[i]], z_recv.at[PLACE[4], i])
                tokens_along_x(4, i)
        for d in group(g):
            to_core(d, 0)
        for d in group(g):
            for i in range(3):
                wait((rb.at[0, k_rows()], sb.at[0, scale_row()], idb.at[0])[i], rz_recv.at[i, PLACE[d]])
            s = 1 if d < 0 else -1
            if g < 3 or d == -3:
                right_along_z(d, s)
        right_along_x(g)
        for d in group(g + 1) if g < 4 else ():
            exchange_weights(d)
        if g > 1:
            for d in group(g - 1):
                pass_tokens(d)
            pass_right(g - 1)
        if g == 3:
            loads[7].wait()
            await_weights(0)
            await_weights(1)
            await_tokens(1)
            multiply((0, 1, 2), 0, 384)
        if g == 4:
            spread_documents()
            await_weights(2)
            await_tokens(2)
            multiply((0, 1, 2), 384, 256)
            multiply((3, 4), 0, 640)
        for d in group(g - 1):
            pass_weights(d)
        if g == 1:
            pass_right(0)
        for i in range(2):
            for d in group(g):
                wait(wb.at[dp, upper], w_recv.at[PLACE[d], i])
                weights_along_y(d, i)
        if g > 1:
            for d in group(g - 1):
                swap_cores(d)
        if g > 1:
            swap_right(g - 2)
    pass_tokens(4)
    pass_right(4)
    swap_right(3)
    await_weights(3)
    multiply((5, 6), 0, 640)
    pass_weights(4)
    await_tokens(3)
    multiply((0, 1, 2, 3, 4, 5, 6), 640, 256)
    swap_cores(4)
    swap_right(4)
    for g in range(5):
        wait(rb.at[places(g), pl.ds(0, 256)], rc_recv.at[0, g])
        wait(sb.at[places(g), pl.ds(0, 4)], rc_recv.at[1, g])
    loads[6].wait()
    await_tokens(4)
    multiply((0, 1, 2, 3, 4, 5, 6), 896, 128)
    await_weights(4)
    multiply((7,), 0, 1024)
    for j in range(4):
        finish(j)

    rest = scores[...]
    columns_sum = jnp.zeros((256, 128), jnp.float32)
    for _ in range(3):
        rounded = rest.astype(jnp.bfloat16)
        rest = rest - rounded.astype(jnp.float32)
        columns_sum += lax.dot_general(spread[...], rounded, NT, preferred_element_type=jnp.float32)
    packed = columns_sum[:32]
    for j in range(1, 8):
        packed += pltpu.roll(columns_sum[j * 32:(j + 1) * 32], j * 16, 1)
    for k in range(32):
        part[k] = packed[k:k + 1]

    def hops(dy, dz):
        return min(dy, NY - dy) + min(dz, NZ - dz)

    offsets = [(dy, dz) for dy in range(NY) for dz in range(NZ) if dy + dz]
    for dy, dz in sorted(offsets, key=lambda o: -hops(*o)):
        send(part.at[window(dz, dy)], got.at[dp], tail_send.at[0], tail_recv.at[0], dy=dy, dz=dz)
    wait(got.at[pl.ds(0, 31)], tail_recv.at[0])
    got[dp] = part[dp]
    tile[...] = jnp.sum(got[...], axis=0)
    for dx, dc in ((2, 1), (2, 0), (1, 1), (3, 1), (1, 0), (3, 0), (0, 1)):
        send(tile, tiles.at[hid], tail_send.at[1], tail_recv.at[1], dx=dx, dc=dc)
    wait(tiles.at[pl.ds(0, hidden_count - 1)], tail_recv.at[1])
    tiles[hid] = tile[...]
    total = jnp.sum(tiles[...], axis=0)
    lane = lax.broadcasted_iota(jnp.int32, (8, 128), 1)
    row = lax.broadcasted_iota(jnp.int32, (8, 128), 0)
    mine = jnp.where((lane & 15) == row + 2 * hid, jnp.broadcast_to(total, (8, 128)), 0.0)
    pick = (lax.shift_right_logical(lane, 4) == row).astype(jnp.float32)
    result = lax.dot_general(
        mine, pick, NT, precision=lax.Precision.HIGHEST, preferred_element_type=jnp.float32
    )
    out[...] = result[:2]

    wait(tok.at[pl.ds(0, 7 * 16)], z_send)
    wait(tok.at[pl.ds(0, 7 * 48)], x_send)
    wait(tok.at[pl.ds(0, 7 * 64)], c_send.at[0])
    wait(rb.at[:, pl.ds(0, 256)], c_send.at[1])
    wait(sb.at[:, pl.ds(0, 4)], c_send.at[2])
    wait(wb.at[pl.ds(0, 7)], w_send)
    wait(wb.at[pl.ds(0, 24)], y_send)
    wait(rb.at[pl.ds(0, 7), pl.ds(0, 64)], r_send.at[0])
    wait(sb.at[pl.ds(0, 7), pl.ds(0, 1)], r_send.at[1])
    wait(idb.at[pl.ds(0, 7)], r_send.at[2])
    wait(rb.at[:, pl.ds(0, 128)], r_send.at[3])
    wait(sb.at[:, pl.ds(0, 2)], r_send.at[4])
    wait(rb.at[:, pl.ds(0, 64)], r_send.at[5])
    wait(sb.at[:, pl.ds(0, 1)], r_send.at[6])
    wait(got.at[pl.ds(0, 31)], tail_send.at[0])
    wait(tiles.at[pl.ds(0, hidden_count - 1)], tail_send.at[1])


def local(tokens, gate_weight, up_weight, cotangent, query_left, query_right, doc_ids, doc_slot):
    bf16, f32, i32 = jnp.bfloat16, jnp.float32, jnp.int32
    dma = pltpu.SemaphoreType.DMA
    anywhere = pl.BlockSpec(memory_space=pltpu.HBM)
    return pl.pallas_call(
        kernel,
        out_shape=jax.ShapeDtypeStruct((2, 8), f32),
        in_specs=[anywhere] * 8,
        out_specs=pl.BlockSpec(memory_space=pltpu.VMEM),
        scratch_shapes=[
            pltpu.VMEM((1024, 4096), bf16),
            pltpu.VMEM((32, 2 * F, 128), bf16),
            pltpu.VMEM((8, 512, 128), jnp.int16),
            pltpu.VMEM((8, 8, 1, 128), f32),
            pltpu.VMEM((8, 1, 128), i32),
            pltpu.VMEM((128, 1792), bf16),
            pltpu.VMEM((128, 1792), bf16),
            pltpu.VMEM((1792, 128), bf16),
            pltpu.VMEM((1792, 128), bf16),
            pltpu.VMEM((128, 4096), bf16),
            pltpu.VMEM((64, 4096), bf16),
            pltpu.VMEM((512, 384), bf16),
            pltpu.VMEM((1, 128), i32),
            pltpu.VMEM((1, 256), i32),
            pltpu.VMEM((2 * F, 1024), f32),
            pltpu.VMEM((384, 1024), bf16),
            pltpu.VMEM((128, 1024), f32),
            pltpu.VMEM((256, 1024), bf16),
            pltpu.VMEM((32, 1, 128), f32),
            pltpu.VMEM((32, 1, 128), f32),
            pltpu.VMEM((1, 128), f32),
            pltpu.VMEM((8, 1, 128), f32),
            dma((8,)), dma, dma, dma((3,)), dma, dma, dma((7,)), dma((2,)),
            dma((8, 2)), dma((8, 2, 2)), dma((8, 2)), dma((8,)), dma((8, 2)), dma((8, 2, 2)), dma((8, 2)),
            dma((3, 8)), dma((2, 5, 2)), dma((3, 5)), dma((2, 5)), dma((2,)),
        ],
        compiler_params=pltpu.CompilerParams(
            collective_id=0, has_side_effects=True, vmem_limit_bytes=60 * 1024 * 1024
        ),
        name="influence",
    )(
        tokens, gate_weight, up_weight, cotangent, query_left, query_right,
        doc_ids.reshape(1, -1), doc_slot.reshape(1, -1),
    )


def solution(mesh):
    return jax.shard_map(
        local,
        mesh=mesh,
        in_specs=(
            P("dp", None),
            P("dp", "hidden"),
            P("dp", "hidden"),
            P("dp", None),
            P(None, "hidden"),
            P("hidden", None),
            P("dp"),
            P(),
        ),
        out_specs=P("hidden", "dp"),
        check_vma=False,
    )
```

```python
import jax
import jax.numpy as jnp
from jax import lax
from jax.experimental import pallas as pl
from jax.experimental.pallas import tpu as pltpu
from jax.sharding import PartitionSpec as P

MESH = pl.DeviceIdType.MESH
NT = (((1,), (1,)), ((), ()))
NX, NY, NZ = 4, 4, 8
R = 32
F = 224
DIST = (0, -1, 1, -2, 2, -3, 3, 4)
PLACE = {d: i for i, d in enumerate(DIST)}
PLACE[-4] = PLACE[4]


def kernel(
    tokens, gate, up, cot, ql, qr, ids, slot, out,
    tok, wb, rb, sb, idb, gate_v, up_v, gate_t, up_t, cot_v, qr_v, ql_v, ids_v, slot_v,
    acc, act, scores, spread, part, got, tile, tiles,
    local_sem, z_send, x_send, c_send, w_send, y_send, r_send, tail_send,
    z_recv, x_recv, xh_recv, c_recv, w_recv, y_recv, yh_recv,
    rz_recv, rx_recv, rxh_recv, rc_recv, tail_recv,
):
    dp, hid = lax.axis_index("dp"), lax.axis_index("hidden")
    y, z = dp // NZ, lax.rem(dp, NZ)
    x, c = hid // 2, lax.rem(hid, 2)
    hidden_count = 2 * NX

    def at(dx=0, dy=0, dz=0, dc=0):
        return (
            lax.rem(y + dy + NY, NY) * NZ + lax.rem(z + dz + NZ, NZ),
            lax.rem(x + dx + NX, NX) * 2 + lax.rem(c + dc, 2),
        )

    def send(src, dst, send_sem, recv_sem, **where):
        pltpu.make_async_remote_copy(
            src, dst, send_sem, recv_sem, device_id=at(**where), device_id_type=MESH
        ).start()

    def wait(ref, sem):
        pltpu.make_async_copy(ref, ref, sem).wait()

    loads = [
        pltpu.make_async_copy(gate, gate_v, local_sem.at[0]),
        pltpu.make_async_copy(up, up_v, local_sem.at[1]),
        pltpu.make_async_copy(cot, cot_v, local_sem.at[2]),
        pltpu.make_async_copy(qr, qr_v, local_sem.at[3]),
        pltpu.make_async_copy(ids, ids_v, local_sem.at[4]),
        pltpu.make_async_copy(slot, slot_v, local_sem.at[5]),
        pltpu.make_async_copy(
            ql.at[:, pl.ds(pl.multiple_of((5 * z) // 3 * 128, 128), 384)], ql_v, local_sem.at[6]
        ),
        pltpu.make_async_copy(tokens, tok.at[pl.ds(0, 128)], local_sem.at[7]),
    ]
    for load in loads:
        load.start()

    barrier = pltpu.get_barrier_semaphore()
    peers = [dict(dz=1), dict(dz=-1), dict(dx=1), dict(dx=-1), dict(dy=1), dict(dy=-1), dict(dc=1)]
    for peer in peers:
        pl.semaphore_signal(barrier, inc=1, device_id=at(**peer), device_id_type=MESH)
    pl.semaphore_wait(barrier, len(peers))

    def rows(d, dx=0):
        first = c * 64 + lax.rem(x + dx + NX, NX) * 16
        return pl.ds(pl.multiple_of(PLACE[d] * 128 + first, 16), 16)

    half = (pl.ds(0, 2048), pl.ds(2048, 2048))
    own_rows = pl.ds(pl.multiple_of(c * 64 + x * 16, 16), 16)
    for i in range(2):
        for s in (1, -1):
            send(
                tokens.at[own_rows, half[i]], tok.at[rows(-s), half[i]], z_send,
                z_recv.at[PLACE[-s], i], dz=s,
            )

    loads[2].wait()
    loads[3].wait()

    def k_rows(dx=0, first=0, count=64):
        start = c * 256 + lax.rem(x + dx + NX, NX) * 64 + first
        return pl.ds(pl.multiple_of(start, count), count)

    def scale_row(dx=0):
        return pl.ds(c * 4 + lax.rem(x + dx + NX, NX), 1)

    right = lax.dot_general(qr_v[...], cot_v[...], NT, preferred_element_type=jnp.float32)
    largest = jnp.maximum(jnp.max(jnp.abs(right), axis=0, keepdims=True), 1e-30)
    steps = right * (32000.0 / largest)
    steps = steps + jnp.where(steps >= 0, 0.5, -0.5)
    rb[0, k_rows(), :] = steps.astype(jnp.int32).astype(jnp.int16)
    sb[0, c * 4 + x] = largest / 32000.0
    loads[4].wait()
    idb[0] = ids_v[...]

    def right_along_z(d, s):
        to = PLACE[d - s]
        here = PLACE[d]
        send(rb.at[here, k_rows()], rb.at[to, k_rows()], r_send.at[0], rz_recv.at[0, to], dz=s)
        send(sb.at[here, scale_row()], sb.at[to, scale_row()], r_send.at[1], rz_recv.at[1, to], dz=s)
        send(idb.at[here], idb.at[to], r_send.at[2], rz_recv.at[2, to], dz=s)

    def group(g):
        return (0,) if g == 0 else (4,) if g == 4 else (-g, g)

    def places(g):
        return pl.ds(PLACE[group(g)[0]], len(group(g)))

    def right_along_x(g):
        for s in (1, -1):
            i = (1 - s) // 2
            mine = rb.at[places(g), k_rows()]
            send(mine, mine, r_send.at[3], rx_recv.at[0, g, i], dx=s)
            mine = sb.at[places(g), scale_row()]
            send(mine, mine, r_send.at[4], rx_recv.at[1, g, i], dx=s)

    def pass_right(g):
        for s in (1, -1):
            i = (1 - s) // 2
            wait(rb.at[places(g), k_rows(-s)], rx_recv.at[0, g, i])
            wait(sb.at[places(g), scale_row(-s)], rx_recv.at[1, g, i])
            piece = rb.at[places(g), k_rows(-s, 32 * i, 32)]
            send(piece, piece, r_send.at[5], rxh_recv.at[i, g], dx=s)
        piece = sb.at[places(g), scale_row(-1)]
        send(piece, piece, r_send.at[6], rxh_recv.at[2, g], dx=1)

    def swap_right(g):
        for i in range(2):
            wait(rb.at[places(g), k_rows(2, 32 * i, 32)], rxh_recv.at[i, g])
        wait(sb.at[places(g), scale_row(2)], rxh_recv.at[2, g])
        mine = rb.at[places(g), pl.ds(pl.multiple_of(c * 256, 256), 256)]
        send(mine, mine, c_send.at[1], rc_recv.at[0, g], dc=1)
        mine = sb.at[places(g), pl.ds(c * 4, 4)]
        send(mine, mine, c_send.at[2], rc_recv.at[1, g], dc=1)

    for s in (1, -1):
        right_along_z(0, s)

    loads[0].wait()
    loads[1].wait()

    @pl.loop(0, 14)
    def _(i):
        at_tile = pl.ds(pl.multiple_of(i * 128, 128), 128)
        gate_t[at_tile, :] = gate_v[:, at_tile].T
        up_t[at_tile, :] = up_v[:, at_tile].T

    def window(dz=0, dy=0):
        return lax.rem(y + dy + NY, NY) * NZ + lax.rem(z + dz + NZ, NZ)

    def units(dz):
        return pl.ds(pl.multiple_of(lax.rem(z + dz + NZ, NZ) * F, 32), F)

    upper, lower = pl.ds(0, F), pl.ds(F, F)

    def exchange_weights(d):
        send(gate_t.at[units(d)], wb.at[dp, upper], w_send, w_recv.at[PLACE[-d], 0], dz=d)
        send(up_t.at[units(d)], wb.at[dp, lower], w_send, w_recv.at[PLACE[-d], 1], dz=d)

    def order(s):
        return (0, 1) if s == 1 else (1, 0)

    parts = (upper, lower)
    for s in (1, -1):
        for i in order(s):
            piece = (gate_t, up_t)[i].at[units(0)]
            send(piece, wb.at[dp, parts[i]], y_send, y_recv.at[0, (1 - s) // 2, i], dy=s)
    for d in (1, -1):
        exchange_weights(d)
    wb[dp, upper, :] = gate_t[units(0), :]
    wb[dp, lower, :] = up_t[units(0), :]

    def tokens_along_x(d, i):
        piece = tok.at[rows(d), half[i]]
        for s in (1, -1):
            send(piece, piece, x_send, x_recv.at[PLACE[d], (1 - s) // 2, i], dx=s)

    def to_core(d, dx):
        piece = tok.at[rows(d, dx)]
        send(piece, piece, c_send.at[0], c_recv.at[PLACE[d]], dc=1)

    def pass_tokens(d):
        for s in (1, -1):
            i = (1 - s) // 2
            wait(tok.at[rows(d), half[i]], x_recv.at[PLACE[d], i, i])
            piece = tok.at[rows(d, -s), half[i]]
            send(piece, piece, x_send, xh_recv.at[PLACE[d], i], dx=s)
        for s in (1, -1):
            i = (1 - s) // 2
            wait(tok.at[rows(d), half[i]], x_recv.at[PLACE[d], i, 1 - i])
            to_core(d, -s)

    def swap_cores(d):
        for i in range(2):
            wait(tok.at[rows(d), half[i]], xh_recv.at[PLACE[d], i])
        to_core(d, 2)

    def weights_along_y(d, i):
        piece = wb.at[window(d), parts[i]]
        for s in (1, -1):
            send(piece, piece, y_send, y_recv.at[PLACE[d], (1 - s) // 2, i], dy=s)

    def pass_weights(d):
        for s in (1, -1):
            i = (1 - s) // 2
            wait(wb.at[dp, upper], y_recv.at[PLACE[d], i, i])
            piece = wb.at[window(d, -s), parts[i]]
            send(piece, piece, y_send, yh_recv.at[PLACE[d], i], dy=s)

    def spread_documents():
        loads[5].wait()
        row = lax.broadcasted_iota(jnp.int32, (256, 256), 0)
        columns = (row & 31) * 8 + lax.shift_right_logical(row, 5)
        placing = (columns == slot_v[...]).astype(jnp.float32).astype(jnp.bfloat16)
        docs = lax.broadcasted_iota(jnp.int32, (256, 128), 0)
        for place in range(NZ):
            one_hot = (docs == idb[place]).astype(jnp.float32).astype(jnp.bfloat16)
            spread[:, pl.ds(place * 128, 128)] = jnp.dot(
                placing, one_hot, preferred_element_type=jnp.float32
            ).astype(jnp.bfloat16)

    def multiply(taken, first, count):
        blocks = [lax.rem(z + DIST[place] + NZ, NZ) for place in taken]
        blocks = [i * NZ + block for block in blocks for i in range(NY)]
        span = pl.ds(first, count)
        weights = jnp.concatenate([wb[block] for block in blocks], axis=1)
        lanes = [pl.ds(pl.multiple_of(block * 128, 128), 128) for block in blocks]
        inputs = jnp.concatenate([tok[span, lane] for lane in lanes], axis=1)
        product = lax.dot_general(weights, inputs, NT, preferred_element_type=jnp.float32)
        acc[:, span] = product if 0 in taken else acc[:, span] + product

    def await_tokens(g):
        for d in group(g):
            wait(tok.at[pl.ds(0, 64)], c_recv.at[PLACE[d]])

    def await_weights(g):
        for d in group(g):
            for i in range(2):
                wait(wb.at[dp, upper], y_recv.at[PLACE[d], i, 1 - i])
                wait(wb.at[dp, upper], yh_recv.at[PLACE[d], i])

    def finish(j):
        span = pl.ds(j * 256, 256)
        gates = acc[:F, span]
        act[pl.ds(first, F), span] = (gates / (1.0 + jnp.exp(-gates)) * acc[F:, span]).astype(jnp.bfloat16)
        left = jnp.dot(ql_v[...], act[:, span], preferred_element_type=jnp.float32)
        for q in range(16):
            hidden = q // 2
            at_row = hidden % 2 * 256 + hidden // 2 * 64 + q % 2 * R
            right = [
                rb[2 * j + i, at_row:at_row + R].astype(jnp.int32).astype(jnp.float32)
                * sb[2 * j + i, hidden % 2 * 4 + hidden // 2]
                for i in range(2)
            ]
            scores[q:q + 1, span] = jnp.sum(
                left[q * R:(q + 1) * R] * jnp.concatenate(right, axis=1), axis=0, keepdims=True
            )

    right_along_x(0)
    act[...] = jnp.zeros_like(act)
    first = pl.multiple_of(F * z - (5 * z) // 3 * 128, 32)
    for g in range(1, 5):
        if g < 4:
            for i in range(2):
                for d in group(g):
                    s = 1 if d < 0 else -1
                    place = PLACE[d]
                    wait(tok.at[rows(d), half[i]], z_recv.at[place, i])
                    if g < 3 or s == 1 - 2 * i:
                        piece = tok.at[rows(d), half[i]]
                        send(piece, tok.at[rows(d - s), half[i]], z_send, z_recv.at[PLACE[d - s], i], dz=s)
                    tokens_along_x(d, i)
        else:
            for i in range(2):
                wait(tok.at[rows(4), half[i]], z_recv.at[PLACE[4], i])
                tokens_along_x(4, i)
        for d in group(g):
            to_core(d, 0)
        for d in group(g):
            for i in range(3):
                wait((rb.at[0, k_rows()], sb.at[0, scale_row()], idb.at[0])[i], rz_recv.at[i, PLACE[d]])
            s = 1 if d < 0 else -1
            if g < 3 or d == -3:
                right_along_z(d, s)
        right_along_x(g)
        for d in group(g + 1) if g < 4 else ():
            exchange_weights(d)
        if g > 1:
            for d in group(g - 1):
                pass_tokens(d)
            pass_right(g - 1)
        if g == 3:
            loads[7].wait()
            await_weights(0)
            await_weights(1)
            await_tokens(1)
            multiply((0, 1, 2), 0, 384)
        if g == 4:
            spread_documents()
            await_weights(2)
            await_tokens(2)
            multiply((0, 1, 2), 384, 256)
            multiply((3, 4), 0, 640)
        for d in group(g - 1):
            pass_weights(d)
        if g == 1:
            pass_right(0)
        for i in range(2):
            for d in group(g):
                wait(wb.at[dp, upper], w_recv.at[PLACE[d], i])
                weights_along_y(d, i)
        if g > 1:
            for d in group(g - 1):
                swap_cores(d)
        if g > 1:
            swap_right(g - 2)
    pass_tokens(4)
    pass_right(4)
    swap_right(3)
    await_weights(3)
    multiply((5, 6), 0, 640)
    pass_weights(4)
    await_tokens(3)
    multiply((0, 1, 2, 3, 4, 5, 6), 640, 256)
    swap_cores(4)
    swap_right(4)
    for g in range(5):
        wait(rb.at[places(g), pl.ds(0, 256)], rc_recv.at[0, g])
        wait(sb.at[places(g), pl.ds(0, 4)], rc_recv.at[1, g])
    loads[6].wait()
    await_tokens(4)
    multiply((0, 1, 2, 3, 4, 5, 6), 896, 128)
    await_weights(4)
    multiply((7,), 0, 1024)
    for j in range(4):
        finish(j)

    rest = scores[:16]
    rounded = []
    for _ in range(3):
        rounded.append(rest.astype(jnp.bfloat16))
        rest = rest - rounded[-1].astype(jnp.float32)
    rounded.append(jnp.zeros((80, 1024), jnp.bfloat16))
    columns_sum = lax.dot_general(
        spread[...], jnp.concatenate(rounded, axis=0), NT, preferred_element_type=jnp.float32
    )
    lane = lax.broadcasted_iota(jnp.int32, (256, 128), 1)
    columns_sum += pltpu.roll(columns_sum, 112, 1) + pltpu.roll(columns_sum, 96, 1)
    columns_sum = jnp.where(lane < 16, columns_sum, 0.0)
    packed = columns_sum[:32]
    for j in range(1, 8):
        packed += pltpu.roll(columns_sum[j * 32:(j + 1) * 32], j * 16, 1)
    for k in range(32):
        part[k] = packed[k:k + 1]

    def hops(dy, dz):
        return min(dy, NY - dy) + min(dz, NZ - dz)

    offsets = [(dy, dz) for dy in range(NY) for dz in range(NZ) if dy + dz]
    for dy, dz in sorted(offsets, key=lambda o: -hops(*o)):
        send(part.at[window(dz, dy)], got.at[dp], tail_send.at[0], tail_recv.at[0], dy=dy, dz=dz)
    wait(got.at[pl.ds(0, 31)], tail_recv.at[0])
    got[dp] = part[dp]
    tile[...] = jnp.sum(got[...], axis=0)
    for dx, dc in ((2, 1), (2, 0), (1, 1), (3, 1), (1, 0), (3, 0), (0, 1)):
        send(tile, tiles.at[hid], tail_send.at[1], tail_recv.at[1], dx=dx, dc=dc)
    wait(tiles.at[pl.ds(0, hidden_count - 1)], tail_recv.at[1])
    tiles[hid] = tile[...]
    total = jnp.sum(tiles[...], axis=0)
    lane = lax.broadcasted_iota(jnp.int32, (8, 128), 1)
    row = lax.broadcasted_iota(jnp.int32, (8, 128), 0)
    mine = jnp.where((lane & 15) == row + 2 * hid, jnp.broadcast_to(total, (8, 128)), 0.0)
    pick = (lax.shift_right_logical(lane, 4) == row).astype(jnp.float32)
    result = lax.dot_general(
        mine, pick, NT, precision=lax.Precision.HIGHEST, preferred_element_type=jnp.float32
    )
    out[...] = result[:2]

    wait(tok.at[pl.ds(0, 7 * 16)], z_send)
    wait(tok.at[pl.ds(0, 7 * 48)], x_send)
    wait(tok.at[pl.ds(0, 7 * 64)], c_send.at[0])
    wait(rb.at[:, pl.ds(0, 256)], c_send.at[1])
    wait(sb.at[:, pl.ds(0, 4)], c_send.at[2])
    wait(wb.at[pl.ds(0, 7)], w_send)
    wait(wb.at[pl.ds(0, 24)], y_send)
    wait(rb.at[pl.ds(0, 7), pl.ds(0, 64)], r_send.at[0])
    wait(sb.at[pl.ds(0, 7), pl.ds(0, 1)], r_send.at[1])
    wait(idb.at[pl.ds(0, 7)], r_send.at[2])
    wait(rb.at[:, pl.ds(0, 128)], r_send.at[3])
    wait(sb.at[:, pl.ds(0, 2)], r_send.at[4])
    wait(rb.at[:, pl.ds(0, 64)], r_send.at[5])
    wait(sb.at[:, pl.ds(0, 1)], r_send.at[6])
    wait(got.at[pl.ds(0, 31)], tail_send.at[0])
    wait(tiles.at[pl.ds(0, hidden_count - 1)], tail_send.at[1])


def local(tokens, gate_weight, up_weight, cotangent, query_left, query_right, doc_ids, doc_slot):
    bf16, f32, i32 = jnp.bfloat16, jnp.float32, jnp.int32
    dma = pltpu.SemaphoreType.DMA
    anywhere = pl.BlockSpec(memory_space=pltpu.HBM)
    return pl.pallas_call(
        kernel,
        out_shape=jax.ShapeDtypeStruct((2, 8), f32),
        in_specs=[anywhere] * 8,
        out_specs=pl.BlockSpec(memory_space=pltpu.VMEM),
        scratch_shapes=[
            pltpu.VMEM((1024, 4096), bf16),
            pltpu.VMEM((32, 2 * F, 128), bf16),
            pltpu.VMEM((8, 512, 128), jnp.int16),
            pltpu.VMEM((8, 8, 1, 128), f32),
            pltpu.VMEM((8, 1, 128), i32),
            pltpu.VMEM((128, 1792), bf16),
            pltpu.VMEM((128, 1792), bf16),
            pltpu.VMEM((1792, 128), bf16),
            pltpu.VMEM((1792, 128), bf16),
            pltpu.VMEM((128, 4096), bf16),
            pltpu.VMEM((64, 4096), bf16),
            pltpu.VMEM((512, 384), bf16),
            pltpu.VMEM((1, 128), i32),
            pltpu.VMEM((1, 256), i32),
            pltpu.VMEM((2 * F, 1024), f32),
            pltpu.VMEM((384, 1024), bf16),
            pltpu.VMEM((16, 1024), f32),
            pltpu.VMEM((256, 1024), bf16),
            pltpu.VMEM((32, 1, 128), f32),
            pltpu.VMEM((32, 1, 128), f32),
            pltpu.VMEM((1, 128), f32),
            pltpu.VMEM((8, 1, 128), f32),
            dma((8,)), dma, dma, dma((3,)), dma, dma, dma((7,)), dma((2,)),
            dma((8, 2)), dma((8, 2, 2)), dma((8, 2)), dma((8,)), dma((8, 2)), dma((8, 2, 2)), dma((8, 2)),
            dma((3, 8)), dma((2, 5, 2)), dma((3, 5)), dma((2, 5)), dma((2,)),
        ],
        compiler_params=pltpu.CompilerParams(
            collective_id=0, has_side_effects=True, vmem_limit_bytes=60 * 1024 * 1024
        ),
        name="influence",
    )(
        tokens, gate_weight, up_weight, cotangent, query_left, query_right,
        doc_ids.reshape(1, -1), doc_slot.reshape(1, -1),
    )


def solution(mesh):
    return jax.shard_map(
        local,
        mesh=mesh,
        in_specs=(
            P("dp", None),
            P("dp", "hidden"),
            P("dp", "hidden"),
            P("dp", None),
            P(None, "hidden"),
            P("hidden", None),
            P("dp"),
            P(),
        ),
        out_specs=P("hidden", "dp"),
        check_vma=False,
    )
```
